512 devices in a mesh: gx: 32 (over y_hi, z, core), gz: 16 (over x, y_lo).
Axes of the slice: x: 4, y: 8 (y_hi: 2, y_lo: 4; y = y_hi * 4 + y_lo), z: 8, core: 2. Of those that a mesh axis runs over, the one named last changes fastest.
Arguments:
- u_field: float32 [2, 8192, 2048], P(None, 'gx', 'gz'), may hold values from -6 to 6
- w_field: float32 [2, 8192, 2048], P(None, 'gx', 'gz'), may hold values from -6 to 6
- temp_field: float32 [2, 8192, 2048], P(None, 'gx', 'gz'), may hold values from -6 to 6
Outputs:
- temp_tendency: float32 [2, 8192, 2048], P(None, 'gx', 'gz')
The draws below stay inside these ranges and needn't reach their ends.
All inputs are finite; a program needn't handle non-finite values.
Results may differ from the reference program's by a relative error of at most 0.00012.
Values sent between devices are 32-bit elements; how exact they have to be, the bound alone decides.
A program may use at most 128 MiB of HBM per device.

```python
import math
import jax
import jax.numpy as jnp

NX = 8192
YS = 2
NZ = 2048


def steps_of(rng, shape, split, smallest, high):
    gain = 1.0
    for axis_at, shards_of in split:
        heights = jax.random.uniform(jax.random.fold_in(jax.random.fold_in(rng, 6), axis_at), (shards_of,), jnp.float32, smallest / len(split), high / len(split))
        gain = gain * jnp.repeat(jnp.exp(heights), shape[axis_at] // shards_of).reshape((-1,) + (1,) * (len(shape) - 1 - axis_at))
    return gain


def bell_draw(stream_key, shape, deviation, limit, shards=(), kind=jnp.bfloat16):
    loudness = steps_of(stream_key, shape, shards, -0.22, 0.18) if shards else 1.0
    array = jax.random.normal(stream_key, shape, jnp.float32) * deviation * loudness
    return jnp.minimum(jnp.maximum(array, -limit), limit).astype(kind)


def setup_inputs(seed: int = 0) -> dict:
    arg_keys = jax.random.split(jax.random.key(seed), 4)
    return {
        "u_field": bell_draw(arg_keys[0], (YS, NX, NZ), 1.0, 6.0, ((1, 32), (2, 16)), jnp.float32),
        "w_field": bell_draw(arg_keys[1], (YS, NX, NZ), 1.0, 6.0, ((1, 32), (2, 16)), jnp.float32),
        "temp_field": bell_draw(arg_keys[2], (YS, NX, NZ), 1.0, 6.0, ((1, 32), (2, 16)), jnp.float32),
    }


full_turn = 2.0 * math.pi
conduction_coefficient = 0.3


def reference(u_field, w_field, temp_field):
    joined_quantity_arrays = jnp.stack([u_field, w_field, temp_field])
    spectra = jnp.fft.fft(joined_quantity_arrays, axis=2)
    position = jnp.arange(NX, dtype=jnp.int32)
    signed = jnp.where(position < NX // 2, position, position - NX)
    kept_modes = (3 * jnp.abs(signed) <= NX)[:, None]
    wavenumber = (full_turn * signed.astype(jnp.float32) / NX)[:, None]
    filtered = jnp.where(kept_modes, spectra, 0.0)
    point_value_domain = jnp.real(jnp.fft.ifft(filtered, axis=2)).astype(jnp.float32)
    lateral_wind_speed = point_value_domain[0]
    upward_wind_speed = point_value_domain[1]
    current_warmth_profile = point_value_domain[2]
    warmth_transport_modes = jnp.fft.fft(lateral_wind_speed * current_warmth_profile, axis=1)
    tendency_spec = -1j * wavenumber * warmth_transport_modes - conduction_coefficient * wavenumber * wavenumber * filtered[2]
    horizontal = jnp.real(jnp.fft.ifft(tendency_spec, axis=1)).astype(jnp.float32)
    enlarged_transport_samples = jnp.pad(upward_wind_speed * current_warmth_profile, ((0, 0), (0, 0), (1, 1)))
    warmth_enlarged_samples = jnp.pad(current_warmth_profile, ((0, 0), (0, 0), (1, 1)))
    upward_levels_count = -0.5 * (enlarged_transport_samples[:, :, 2:] - enlarged_transport_samples[:, :, :-2])
    upward_levels_count = upward_levels_count + conduction_coefficient * (warmth_enlarged_samples[:, :, 2:] - 2.0 * current_warmth_profile + warmth_enlarged_samples[:, :, :-2])
    return horizontal + upward_levels_count
```

```python
import functools
import math

import jax
import jax.numpy as jnp
import ml_dtypes
import numpy as np
from jax import lax
from jax.experimental import pallas as pl
from jax.experimental.pallas import tpu as pltpu
from jax.sharding import PartitionSpec as P

MESH = pl.DeviceIdType.MESH
conduction = 0.3
HALF = 128


def split_np(a):
    a32 = a.astype(np.float32)
    hi = a32.astype(ml_dtypes.bfloat16)
    lo = (a - hi.astype(np.float64)).astype(np.float32).astype(ml_dtypes.bfloat16)
    return hi, lo


@functools.lru_cache(maxsize=None)
def tables(n_dev, n_loc):
    total = n_dev * n_loc
    d = np.arange(n_dev)
    turn = -2.0 * np.pi * (np.outer(d, d) % n_dev) / n_dev
    c, s = np.cos(turn), np.sin(turn)
    outer = np.zeros((2, n_dev, 4, n_dev, 2, 4))
    for q in range(4):
        outer[0, :, q, :, 0, q] = c
        outer[0, :, q, :, 1, q] = -s
        outer[1, :, q, :, 0, q] = s
        outer[1, :, q, :, 1, q] = c
    outer = outer.reshape(8 * n_dev, 8 * n_dev)
    outer_inv = outer.T / n_dev
    j = np.arange(n_loc)
    turn = -2.0 * np.pi * (np.outer(j, j) % n_loc) / n_loc
    c, s = np.cos(turn), np.sin(turn)
    inner = np.block([[c, s], [-s, c]])
    inner_inv = inner.T / n_loc
    ka = np.repeat(d, 4)
    turn = -2.0 * np.pi * np.outer(ka, j) / total
    k = ka[:, None] + n_dev * j[None, :]
    signed = np.where(k < total // 2, k, k - total)
    kept = 3 * np.abs(signed) <= total
    wave = 2.0 * np.pi * signed / total
    first = np.where(2 * k == total, 0.0, wave)
    second = conduction * wave * wave * kept
    f32 = np.stack([np.cos(turn), np.sin(turn), kept, first, second]).astype(np.float32)
    mats = []
    for m in (outer, outer_inv):
        mats += split_np(m)
    big = []
    for m in (inner, inner_inv):
        big += split_np(m)
    return f32, np.stack(mats), np.stack(big)


def split(a):
    hi = a.astype(jnp.bfloat16)
    lo = (a - hi.astype(jnp.float32)).astype(jnp.bfloat16)
    return hi, lo


def dot(a, b):
    return jnp.dot(a, b, preferred_element_type=jnp.float32)


def kernel(
    n, layers,
    u_ref, w_ref, t_ref, f32_hbm, mats_hbm, big_hbm,
    out_ref,
    tab, mats, big, sbuf, rbuf, obuf, sspec, uphys, tphys, edge_s, edge_r,
    const_sem, send_sem, recv_sem, osend_sem, orecv_sem, esend_sem, erecv_sem,
):
    me = lax.axis_index("gx")
    lay = lax.axis_index("gz")
    blocks = n // 2
    b = lax.rem(me, blocks)
    base = me - b
    consts = [
        pltpu.make_async_copy(src, dst, const_sem.at[i])
        for i, (src, dst) in enumerate(((f32_hbm, tab), (mats_hbm, mats), (big_hbm, big)))
    ]
    for c in consts:
        c.start()
    nxt_gx = base + lax.rem(b + 1, blocks)
    nxt_gz = lax.rem(lay + jnp.where(b == blocks - 1, 1, 0), layers)
    prv_gx = base + lax.rem(b + blocks - 1, blocks)
    prv_gz = lax.rem(lay + jnp.where(b == 0, layers - 1, 0), layers)

    barrier = pltpu.get_barrier_semaphore()

    def greet(i, carry):
        pl.semaphore_signal(barrier, inc=1, device_id=(lax.rem(me + i, n), lay), device_id_type=MESH)
        return carry

    lax.fori_loop(1, n, greet, 0)
    pl.semaphore_signal(barrier, inc=1, device_id=(nxt_gx, nxt_gz), device_id_type=MESH)
    pl.semaphore_signal(barrier, inc=1, device_id=(prv_gx, prv_gz), device_id_type=MESH)

    def turned(src, f):
        for y in range(2):
            sbuf[f, pl.ds(y * blocks, blocks)] = src[y].T.reshape(blocks, 8, src.shape[1])

    def scatter(f):
        def send(i, carry):
            p = lax.rem(me + i, n)
            pltpu.make_async_remote_copy(
                src_ref=sbuf.at[f, p], dst_ref=rbuf.at[f, me],
                send_sem=send_sem.at[f], recv_sem=recv_sem.at[f],
                device_id=(p, lay), device_id_type=MESH,
            ).start()
            return carry

        lax.fori_loop(1, n, send, 0)
        pltpu.make_async_copy(sbuf.at[f, me], rbuf.at[f, me], recv_sem.at[f]).start()

    def gathered(f):
        pltpu.make_async_copy(sbuf.at[f], rbuf.at[f], recv_sem.at[f]).wait()

    turned(t_ref, 0)
    pl.semaphore_wait(barrier, n + 1)
    scatter(0)
    turned(u_ref, 1)
    scatter(1)
    turned(w_ref, 2)
    scatter(2)
    for c in consts:
        c.wait()

    def left(i, x):
        hi, lo = split(x)
        return dot(mats[i], hi) + dot(mats[i + 1], hi) + dot(mats[i], lo)

    def right(i, x):
        hi, lo = split(x)
        return dot(hi, big[i]) + dot(lo, big[i]) + dot(hi, big[i + 1])

    def forward(x):
        a = left(0, x)
        re, im = a[:HALF], a[HALF:]
        c, s = tab[0], tab[1]
        a = jnp.concatenate([re * c - im * s, re * s + im * c], axis=1)
        a = right(0, a)
        w = a.shape[1] // 2
        return a[:, :w], a[:, w:]

    def backward(re, im):
        a = right(2, jnp.concatenate([re, im], axis=1))
        w = a.shape[1] // 2
        re, im = a[:, :w], a[:, w:]
        c, s = tab[0], tab[1]
        a = jnp.concatenate([re * c + im * s, im * c - re * s], axis=0)
        return left(2, a)

    def lines(f):
        return rbuf[f].reshape(8 * n, rbuf.shape[3])

    def edges(i, value):
        v = value.reshape(n, 8, value.shape[1])
        edge_s[i, 0] = v[:, 0]
        edge_s[i, 1] = v[:, 7]

    def edge_copies(i):
        out = []
        for side, (gx, gz) in ((0, (prv_gx, prv_gz)), (1, (nxt_gx, nxt_gz))):
            out.append(pltpu.make_async_remote_copy(
                src_ref=edge_s.at[i, side], dst_ref=edge_r.at[i, side],
                send_sem=esend_sem.at[i, side], recv_sem=erecv_sem.at[i, side],
                device_id=(gx, gz), device_id_type=MESH,
            ))
        return out

    gathered(0)
    re, im = forward(lines(0))
    kept = tab[2]
    re, im = re * kept, im * kept
    sspec[0] = re
    sspec[1] = im
    tp = backward(re, im)
    tphys[...] = tp
    edges(0, tp)
    t_edges = edge_copies(0)
    for c in t_edges:
        c.start()
    gathered(1)
    re, im = forward(lines(1))
    kept = tab[2]
    up = backward(re * kept, im * kept)
    re, im = forward(up * tphys[...])
    first, second = tab[3], tab[4]
    uphys[...] = backward(first * im - second * sspec[0], -first * re - second * sspec[1])
    gathered(2)
    re, im = forward(lines(2))
    kept = tab[2]
    q = backward(re * kept, im * kept) * tphys[...]
    edges(1, q)
    q_edges = edge_copies(1)
    for c in q_edges:
        c.start()
    for c in t_edges + q_edges:
        c.wait()
    has_prev = jnp.where((b == 0) & (lay == 0), 0.0, 1.0).astype(jnp.float32)
    has_next = jnp.where((b == blocks - 1) & (lay == layers - 1), 0.0, 1.0).astype(jnp.float32)
    q3 = q.reshape(n, 8, q.shape[1])
    t3 = tphys[...].reshape(n, 8, q.shape[1])
    lower = jnp.concatenate([(0.5 * q3 + conduction * t3)[:, :7]], axis=1)
    upper = (conduction * t3 - 0.5 * q3)[:, 1:]
    low_edge = has_prev * (0.5 * edge_r[1, 1] + conduction * edge_r[0, 1])
    high_edge = has_next * (conduction * edge_r[0, 0] - 0.5 * edge_r[1, 0])
    h3 = uphys[...].reshape(n, 8, q.shape[1])
    total = h3 - 2.0 * conduction * t3
    total = total + jnp.concatenate([low_edge[:, None], lower], axis=1)
    total = total + jnp.concatenate([upper, high_edge[:, None]], axis=1)
    obuf[...] = total

    def send_back(i, carry):
        p = lax.rem(me + i, n)
        pltpu.make_async_remote_copy(
            src_ref=obuf.at[p], dst_ref=out_ref.at[me],
            send_sem=osend_sem.at[0], recv_sem=orecv_sem.at[0],
            device_id=(p, lay), device_id_type=MESH,
        ).start()
        return carry

    lax.fori_loop(1, n, send_back, 0)
    pltpu.make_async_copy(obuf.at[me], out_ref.at[me], orecv_sem.at[0]).start()
    pltpu.make_async_copy(obuf, out_ref, orecv_sem.at[0]).wait()

    some = pl.ds(0, n - 1)
    for f in range(3):
        pltpu.make_async_copy(sbuf.at[f, some], rbuf.at[f, some], send_sem.at[f]).wait()
    pltpu.make_async_copy(obuf.at[some], out_ref.at[some], osend_sem.at[0]).wait()


def solution(mesh):
    n = mesh.shape["gx"]
    layers = mesh.shape["gz"]

    def shards(u_field, w_field, temp_field):
        ys, nx, nz = u_field.shape
        f32, mats, big = (jnp.asarray(t) for t in tables(n, nx))
        vmem = pl.BlockSpec(memory_space=pltpu.VMEM)
        hbm = pl.BlockSpec(memory_space=pltpu.HBM)
        dma = pltpu.SemaphoreType.DMA
        back = pl.pallas_call(
            functools.partial(kernel, n, layers),
            out_shape=jax.ShapeDtypeStruct((n, 8, nx), jnp.float32),
            in_specs=[vmem] * 3 + [hbm] * 3,
            out_specs=vmem,
            scratch_shapes=[
                pltpu.VMEM(f32.shape, jnp.float32),
                pltpu.VMEM(mats.shape, jnp.bfloat16),
                pltpu.VMEM(big.shape, jnp.bfloat16),
                pltpu.VMEM((3, n, 8, nx), jnp.float32),
                pltpu.VMEM((3, n, 8, nx), jnp.float32),
                pltpu.VMEM((n, 8, nx), jnp.float32),
                pltpu.VMEM((2, HALF, nx), jnp.float32),
                pltpu.VMEM((8 * n, nx), jnp.float32),
                pltpu.VMEM((8 * n, nx), jnp.float32),
                pltpu.VMEM((2, 2, n, nx), jnp.float32),
                pltpu.VMEM((2, 2, n, nx), jnp.float32),
                dma((3,)), dma((3,)), dma((3,)), dma((1,)), dma((1,)), dma((2, 2)), dma((2, 2)),
            ],
            compiler_params=pltpu.CompilerParams(
                collective_id=0, has_side_effects=True, vmem_limit_bytes=40 * 2**20
            ),
        )(u_field, w_field, temp_field, f32, mats, big)
        return jnp.swapaxes(back.reshape(ys, nz, nx), 1, 2)

    spec = P(None, "gx", "gz")
    return jax.shard_map(shards, mesh=mesh, in_specs=(spec, spec, spec), out_specs=spec, check_vma=False)
```

```python
import functools
import math

import jax
import jax.numpy as jnp
import ml_dtypes
import numpy as np
from jax import lax
from jax.experimental import pallas as pl
from jax.experimental.pallas import tpu as pltpu
from jax.sharding import PartitionSpec as P

MESH = pl.DeviceIdType.MESH
conduction = 0.3
HALF = 128


def split_np(a):
    a32 = a.astype(np.float32)
    hi = a32.astype(ml_dtypes.bfloat16)
    lo = (a - hi.astype(np.float64)).astype(np.float32).astype(ml_dtypes.bfloat16)
    return hi, lo


@functools.lru_cache(maxsize=None)
def tables(n_dev, n_loc):
    total = n_dev * n_loc
    d = np.arange(n_dev)
    turn = -2.0 * np.pi * (np.outer(d, d) % n_dev) / n_dev
    c, s = np.cos(turn), np.sin(turn)
    outer = np.zeros((2, n_dev, 4, n_dev, 2, 4))
    for q in range(4):
        outer[0, :, q, :, 0, q] = c
        outer[0, :, q, :, 1, q] = -s
        outer[1, :, q, :, 0, q] = s
        outer[1, :, q, :, 1, q] = c
    outer = outer.reshape(8 * n_dev, 8 * n_dev)
    outer_inv = outer.T / n_dev
    j = np.arange(n_loc)
    turn = -2.0 * np.pi * (np.outer(j, j) % n_loc) / n_loc
    c, s = np.cos(turn), np.sin(turn)
    inner = np.block([[c, s], [-s, c]])
    inner_inv = inner.T / n_loc
    ka = np.repeat(d, 4)
    turn = -2.0 * np.pi * np.outer(ka, j) / total
    k = ka[:, None] + n_dev * j[None, :]
    signed = np.where(k < total // 2, k, k - total)
    kept = 3 * np.abs(signed) <= total
    wave = 2.0 * np.pi * signed / total
    first = np.where(2 * k == total, 0.0, wave)
    second = conduction * wave * wave * kept
    f32 = np.stack([np.cos(turn), np.sin(turn), kept, first, second]).astype(np.float32)
    mats = []
    for m in (outer, outer_inv):
        mats += split_np(m)
    big = []
    for m in (inner, inner_inv):
        big += split_np(m)
    return f32, np.stack(mats), np.stack(big)


def split(a):
    hi = a.astype(jnp.bfloat16)
    lo = (a - hi.astype(jnp.float32)).astype(jnp.bfloat16)
    return hi, lo


def dot(a, b):
    return jnp.dot(a, b, preferred_element_type=jnp.float32)


def kernel(
    n, layers,
    u_hbm, w_hbm, t_hbm, f32_hbm, mats_hbm, big_hbm,
    out_ref,
    fields, tab, mats, big, sbuf, rbuf, obuf, sspec, uphys, tphys, edge_s, edge_r,
    load_sem, const_sem, send_sem, recv_sem, osend_sem, orecv_sem, esend_sem, erecv_sem,
):
    me = lax.axis_index("gx")
    lay = lax.axis_index("gz")
    blocks = n // 2
    b = lax.rem(me, blocks)
    base = me - b
    consts = [
        pltpu.make_async_copy(src, dst, const_sem.at[i])
        for i, (src, dst) in enumerate(((f32_hbm, tab), (mats_hbm, mats), (big_hbm, big)))
    ]
    loads = [
        pltpu.make_async_copy(src, fields.at[f], load_sem.at[f])
        for f, src in enumerate((t_hbm, u_hbm, w_hbm))
    ]
    for c in loads + consts:
        c.start()
    nxt_gx = base + lax.rem(b + 1, blocks)
    nxt_gz = lax.rem(lay + jnp.where(b == blocks - 1, 1, 0), layers)
    prv_gx = base + lax.rem(b + blocks - 1, blocks)
    prv_gz = lax.rem(lay + jnp.where(b == 0, layers - 1, 0), layers)

    barrier = pltpu.get_barrier_semaphore()

    def greet(i, carry):
        pl.semaphore_signal(barrier, inc=1, device_id=(lax.rem(me + i, n), lay), device_id_type=MESH)
        return carry

    lax.fori_loop(1, n, greet, 0)
    pl.semaphore_signal(barrier, inc=1, device_id=(nxt_gx, nxt_gz), device_id_type=MESH)
    pl.semaphore_signal(barrier, inc=1, device_id=(prv_gx, prv_gz), device_id_type=MESH)

    def turned(f):
        loads[f].wait()
        for y in range(2):
            sbuf[f, pl.ds(y * blocks, blocks)] = fields[f, y].T.reshape(blocks, 8, fields.shape[2])

    def scatter(f):
        def send(i, carry):
            p = lax.rem(me + i, n)
            pltpu.make_async_remote_copy(
                src_ref=sbuf.at[f, p], dst_ref=rbuf.at[f, me],
                send_sem=send_sem.at[f], recv_sem=recv_sem.at[f],
                device_id=(p, lay), device_id_type=MESH,
            ).start()
            return carry

        lax.fori_loop(1, n, send, 0)
        pltpu.make_async_copy(sbuf.at[f, me], rbuf.at[f, me], recv_sem.at[f]).start()

    def gathered(f):
        pltpu.make_async_copy(sbuf.at[f], rbuf.at[f], recv_sem.at[f]).wait()

    turned(0)
    pl.semaphore_wait(barrier, n + 1)
    scatter(0)
    turned(1)
    scatter(1)
    turned(2)
    scatter(2)
    for c in consts:
        c.wait()

    def left(i, x):
        hi, lo = split(x)
        return dot(mats[i], hi) + dot(mats[i + 1], hi) + dot(mats[i], lo)

    def right(i, x):
        hi, lo = split(x)
        return dot(hi, big[i]) + dot(lo, big[i]) + dot(hi, big[i + 1])

    def forward(x):
        a = left(0, x)
        re, im = a[:HALF], a[HALF:]
        c, s = tab[0], tab[1]
        a = jnp.concatenate([re * c - im * s, re * s + im * c], axis=1)
        a = right(0, a)
        w = a.shape[1] // 2
        return a[:, :w], a[:, w:]

    def backward(re, im):
        a = right(2, jnp.concatenate([re, im], axis=1))
        w = a.shape[1] // 2
        re, im = a[:, :w], a[:, w:]
        c, s = tab[0], tab[1]
        a = jnp.concatenate([re * c + im * s, im * c - re * s], axis=0)
        return left(2, a)

    def lines(f):
        return rbuf[f].reshape(8 * n, rbuf.shape[3])

    def edges(i, value):
        v = value.reshape(n, 8, value.shape[1])
        edge_s[i, 0] = v[:, 0]
        edge_s[i, 1] = v[:, 7]

    def edge_copies(i):
        out = []
        for side, (gx, gz) in ((0, (prv_gx, prv_gz)), (1, (nxt_gx, nxt_gz))):
            out.append(pltpu.make_async_remote_copy(
                src_ref=edge_s.at[i, side], dst_ref=edge_r.at[i, side],
                send_sem=esend_sem.at[i, side], recv_sem=erecv_sem.at[i, side],
                device_id=(gx, gz), device_id_type=MESH,
            ))
        return out

    gathered(0)
    re, im = forward(lines(0))
    kept = tab[2]
    re, im = re * kept, im * kept
    sspec[0] = re
    sspec[1] = im
    tp = backward(re, im)
    tphys[...] = tp
    edges(0, tp)
    t_edges = edge_copies(0)
    for c in t_edges:
        c.start()
    gathered(1)
    re, im = forward(lines(1))
    kept = tab[2]
    up = backward(re * kept, im * kept)
    re, im = forward(up * tphys[...])
    first, second = tab[3], tab[4]
    uphys[...] = backward(first * im - second * sspec[0], -first * re - second * sspec[1])
    gathered(2)
    re, im = forward(lines(2))
    kept = tab[2]
    q = backward(re * kept, im * kept) * tphys[...]
    edges(1, q)
    q_edges = edge_copies(1)
    for c in q_edges:
        c.start()
    for c in t_edges + q_edges:
        c.wait()
    has_prev = jnp.where((b == 0) & (lay == 0), 0.0, 1.0).astype(jnp.float32)
    has_next = jnp.where((b == blocks - 1) & (lay == layers - 1), 0.0, 1.0).astype(jnp.float32)
    q3 = q.reshape(n, 8, q.shape[1])
    t3 = tphys[...].reshape(n, 8, q.shape[1])
    lower = jnp.concatenate([(0.5 * q3 + conduction * t3)[:, :7]], axis=1)
    upper = (conduction * t3 - 0.5 * q3)[:, 1:]
    low_edge = has_prev * (0.5 * edge_r[1, 1] + conduction * edge_r[0, 1])
    high_edge = has_next * (conduction * edge_r[0, 0] - 0.5 * edge_r[1, 0])
    h3 = uphys[...].reshape(n, 8, q.shape[1])
    total = h3 - 2.0 * conduction * t3
    total = total + jnp.concatenate([low_edge[:, None], lower], axis=1)
    total = total + jnp.concatenate([upper, high_edge[:, None]], axis=1)
    obuf[...] = total

    def send_back(i, carry):
        p = lax.rem(me + i, n)
        pltpu.make_async_remote_copy(
            src_ref=obuf.at[p], dst_ref=out_ref.at[me],
            send_sem=osend_sem.at[0], recv_sem=orecv_sem.at[0],
            device_id=(p, lay), device_id_type=MESH,
        ).start()
        return carry

    lax.fori_loop(1, n, send_back, 0)
    pltpu.make_async_copy(obuf.at[me], out_ref.at[me], orecv_sem.at[0]).start()
    pltpu.make_async_copy(obuf, out_ref, orecv_sem.at[0]).wait()

    some = pl.ds(0, n - 1)
    for f in range(3):
        pltpu.make_async_copy(sbuf.at[f, some], rbuf.at[f, some], send_sem.at[f]).wait()
    pltpu.make_async_copy(obuf.at[some], out_ref.at[some], osend_sem.at[0]).wait()


def solution(mesh):
    n = mesh.shape["gx"]
    layers = mesh.shape["gz"]

    def shards(u_field, w_field, temp_field):
        ys, nx, nz = u_field.shape
        f32, mats, big = (jnp.asarray(t) for t in tables(n, nx))
        vmem = pl.BlockSpec(memory_space=pltpu.VMEM)
        hbm = pl.BlockSpec(memory_space=pltpu.HBM)
        dma = pltpu.SemaphoreType.DMA
        back = pl.pallas_call(
            functools.partial(kernel, n, layers),
            out_shape=jax.ShapeDtypeStruct((n, 8, nx), jnp.float32),
            in_specs=[hbm] * 6,
            out_specs=vmem,
            scratch_shapes=[
                pltpu.VMEM((3, ys, nx, nz), jnp.float32),
                pltpu.VMEM(f32.shape, jnp.float32),
                pltpu.VMEM(mats.shape, jnp.bfloat16),
                pltpu.VMEM(big.shape, jnp.bfloat16),
                pltpu.VMEM((3, n, 8, nx), jnp.float32),
                pltpu.VMEM((3, n, 8, nx), jnp.float32),
                pltpu.VMEM((n, 8, nx), jnp.float32),
                pltpu.VMEM((2, HALF, nx), jnp.float32),
                pltpu.VMEM((8 * n, nx), jnp.float32),
                pltpu.VMEM((8 * n, nx), jnp.float32),
                pltpu.VMEM((2, 2, n, nx), jnp.float32),
                pltpu.VMEM((2, 2, n, nx), jnp.float32),
                dma((3,)), dma((3,)), dma((3,)), dma((3,)), dma((1,)), dma((1,)), dma((2, 2)), dma((2, 2)),
            ],
            compiler_params=pltpu.CompilerParams(
                collective_id=0, has_side_effects=True, vmem_limit_bytes=60 * 2**20
            ),
        )(u_field, w_field, temp_field, f32, mats, big)
        return jnp.swapaxes(back.reshape(ys, nz, nx), 1, 2)

    spec = P(None, "gx", "gz")
    return jax.shard_map(shards, mesh=mesh, in_specs=(spec, spec, spec), out_specs=spec, check_vma=False)
```

```python
import functools
import math

import jax
import jax.numpy as jnp
import ml_dtypes
import numpy as np
from jax import lax
from jax.experimental import pallas as pl
from jax.experimental.pallas import tpu as pltpu
from jax.sharding import PartitionSpec as P

MESH = pl.DeviceIdType.MESH
conduction = 0.3


def split_np(a):
    a32 = a.astype(np.float32)
    hi = a32.astype(ml_dtypes.bfloat16)
    lo = (a - hi.astype(np.float64)).astype(np.float32).astype(ml_dtypes.bfloat16)
    return hi, lo


@functools.lru_cache(maxsize=None)
def tables(n_dev, n_loc):
    total = n_dev * n_loc
    d = np.arange(n_dev)
    k = d[:, None] + n_dev * np.arange(-n_loc // 2, n_loc // 2)[None, :]
    kept = 3 * np.abs(k) <= total
    count = kept.sum(1)
    wide = count.max()
    assert set(count) == {wide, wide - 1}
    order = np.concatenate([d[count == wide], d[count < wide]])
    n_wide = int((count == wide).sum())
    low = np.argmax(kept, axis=1) - n_loc // 2
    centre = low + (count - 1) / 2.0
    turn = -2.0 * np.pi * (np.outer(order, d) % n_dev) / n_dev
    c, s = np.cos(turn), np.sin(turn)
    outer = np.zeros((n_dev, 2, 4, n_dev, 2, 4))
    for q in range(4):
        outer[:, 0, q, :, 0, q] = c
        outer[:, 0, q, :, 1, q] = -s
        outer[:, 1, q, :, 0, q] = s
        outer[:, 1, q, :, 1, q] = c
    outer = outer.reshape(8 * n_dev, 8 * n_dev)
    outer_inv = outer.T / n_dev
    j = np.arange(n_loc)
    apart = 2.0 * np.pi * (j[None, :] - j[:, None]) / n_loc
    step = 2.0 * np.pi / total

    def real_kernels(modes):
        kappa = np.arange(modes) - (modes - 1) / 2.0
        angle = apart[..., None] * kappa
        even = np.cos(angle).sum(-1) / n_loc
        odd = -(kappa * np.sin(angle)).sum(-1) / n_loc
        return even, odd * n_dev * step

    def frame(offset):
        turn = step * np.outer(order + n_dev * offset, j)
        return np.cos(turn), np.sin(turn), np.repeat((order + n_dev * offset)[:, None], n_loc, 1) * step

    def rows(a, signed):
        a = np.repeat(a[:, None, :], 8, axis=1)
        if signed:
            a[:, :4] *= -1.0
        return a.reshape(8 * n_dev, n_loc)

    fc, fs, fa = frame(centre[order])
    dc, ds, da = frame(np.full(n_dev, -0.5))
    f32 = np.stack([
        rows(fc, False), rows(fs, True), conduction * rows(fa, True),
        rows(dc, False), rows(ds, True), rows(da, True),
    ]).astype(np.float32)
    even_w, odd_w = real_kernels(wide)
    even_n, odd_n = real_kernels(wide - 1)
    _, full = real_kernels(n_loc)
    mats = []
    for m in (outer, outer_inv, even_w, conduction * odd_w, even_n, conduction * odd_n, full):
        mats += split_np(m)
    return f32, np.stack(mats), 8 * n_wide


def split(a):
    hi = a.astype(jnp.bfloat16)
    lo = (a - hi.astype(jnp.float32)).astype(jnp.bfloat16)
    return hi, lo


def dot(a, b):
    return jnp.dot(a, b, preferred_element_type=jnp.float32)


def kernel(
    n, layers, cut,
    u_hbm, w_hbm, t_hbm, f32_hbm, mats_hbm,
    out_ref,
    fields, tab, mats, sbuf, rbuf, obuf, grad, tphys, qphys, vert, edge_s, edge_r,
    load_sem, const_sem, send_sem, recv_sem, osend_sem, orecv_sem, esend_sem, erecv_sem,
):
    me = lax.axis_index("gx")
    lay = lax.axis_index("gz")
    blocks = n // 2
    b = lax.rem(me, blocks)
    base = me - b
    consts = [
        pltpu.make_async_copy(src, dst, const_sem.at[i])
        for i, (src, dst) in enumerate(((f32_hbm, tab), (mats_hbm, mats)))
    ]
    loads = [
        pltpu.make_async_copy(src, fields.at[f], load_sem.at[f])
        for f, src in enumerate((t_hbm, w_hbm, u_hbm))
    ]
    for c in loads + consts:
        c.start()
    nxt_gx = base + lax.rem(b + 1, blocks)
    nxt_gz = lax.rem(lay + jnp.where(b == blocks - 1, 1, 0), layers)
    prv_gx = base + lax.rem(b + blocks - 1, blocks)
    prv_gz = lax.rem(lay + jnp.where(b == 0, layers - 1, 0), layers)

    barrier = pltpu.get_barrier_semaphore()

    def greet(i, carry):
        pl.semaphore_signal(barrier, inc=1, device_id=(lax.rem(me + i, n), lay), device_id_type=MESH)
        return carry

    lax.fori_loop(1, n, greet, 0)
    pl.semaphore_signal(barrier, inc=1, device_id=(nxt_gx, nxt_gz), device_id_type=MESH)
    pl.semaphore_signal(barrier, inc=1, device_id=(prv_gx, prv_gz), device_id_type=MESH)

    def turned(f):
        loads[f].wait()
        for y in range(2):
            sbuf[f, pl.ds(y * blocks, blocks)] = fields[f, y].T.reshape(blocks, 8, fields.shape[2])

    def scatter(f):
        def send(i, carry):
            p = lax.rem(me + i, n)
            pltpu.make_async_remote_copy(
                src_ref=sbuf.at[f, p], dst_ref=rbuf.at[f, me],
                send_sem=send_sem.at[f], recv_sem=recv_sem.at[f],
                device_id=(p, lay), device_id_type=MESH,
            ).start()
            return carry

        lax.fori_loop(1, n, send, 0)
        pltpu.make_async_copy(sbuf.at[f, me], rbuf.at[f, me], recv_sem.at[f]).start()

    def gathered(f):
        pltpu.make_async_copy(sbuf.at[f], rbuf.at[f], recv_sem.at[f]).wait()

    turned(0)
    pl.semaphore_wait(barrier, n + 1)
    scatter(0)
    turned(1)
    scatter(1)
    turned(2)
    scatter(2)
    for c in consts:
        c.wait()

    def left(i, x):
        hi, lo = split(x)
        return dot(mats[i], hi) + dot(mats[i + 1], hi) + dot(mats[i], lo)

    def right(i, hi, lo):
        return dot(hi, mats[i]) + dot(lo, mats[i]) + dot(hi, mats[i + 1])

    def swapped(x):
        x3 = x.reshape(n, 8, x.shape[1])
        return jnp.concatenate([x3[:, 4:], x3[:, :4]], axis=1).reshape(x.shape)

    def modulated(x, i):
        return x * tab[i] - swapped(x) * tab[i + 1]

    def demodulated(x, i):
        return x * tab[i] + swapped(x) * tab[i + 1]

    low_cut, high_cut = cut // 16 * 16, -(-cut // 16) * 16

    def by_class(x, i):
        hi, lo = split(x)
        first = right(i, hi[:high_cut], lo[:high_cut])
        second = right(i + 4, hi[low_cut:], lo[low_cut:])
        return jnp.concatenate([first[:cut], second[cut - low_cut:]], axis=0)

    def filtered(x):
        a = modulated(left(0, x), 0)
        return left(2, demodulated(by_class(a, 4), 0))

    def filtered_and_gradient(x):
        a = modulated(left(0, x), 0)
        kept = demodulated(by_class(a, 4), 0)
        slope = demodulated(by_class(a, 6), 0) + swapped(kept) * tab[2]
        both = left(2, jnp.concatenate([kept, slope], axis=1))
        w = both.shape[1] // 2
        return both[:, :w], both[:, w:]

    def gradient(x):
        a = left(0, x)
        hi, lo = split(modulated(a, 3))
        b = demodulated(right(12, hi, lo), 3) + swapped(a) * tab[5]
        lane = lax.broadcasted_iota(jnp.int32, (8, a.shape[1]), 1)
        sign = jnp.where(lane % 2 == 0, 1.0, -1.0).astype(jnp.float32)
        total = jnp.sum(a[:8] * sign, axis=1, keepdims=True) * (math.pi / a.shape[1])
        part = lax.broadcasted_iota(jnp.int32, (8, a.shape[1]), 0)
        total = jnp.broadcast_to(total, sign.shape)
        turned_total = jnp.concatenate([total[4:], total[:4]], axis=0)
        fix = jnp.where(part < 4, -turned_total, turned_total) * sign
        b = jnp.concatenate([b[:8] + fix, b[8:]], axis=0)
        return left(2, b)

    def lines(f):
        return rbuf[f].reshape(8 * n, rbuf.shape[3])

    def edges(i, value):
        v = value.reshape(n, 8, value.shape[1])
        edge_s[i, 0] = v[:, 0]
        edge_s[i, 1] = v[:, 7]

    def edge_copies(i):
        out = []
        for side, (gx, gz) in ((0, (prv_gx, prv_gz)), (1, (nxt_gx, nxt_gz))):
            out.append(pltpu.make_async_remote_copy(
                src_ref=edge_s.at[i, side], dst_ref=edge_r.at[i, side],
                send_sem=esend_sem.at[i, side], recv_sem=erecv_sem.at[i, side],
                device_id=(gx, gz), device_id_type=MESH,
            ))
        return out

    gathered(0)
    tp, slope = filtered_and_gradient(lines(0))
    tphys[...] = tp
    grad[...] = slope
    edges(0, tp)
    t_edges = edge_copies(0)
    for c in t_edges:
        c.start()
    gathered(1)
    q = filtered(lines(1)) * tphys[...]
    qphys[...] = q
    edges(1, q)
    q_edges = edge_copies(1)
    for c in q_edges:
        c.start()
    for c in t_edges + q_edges:
        c.wait()
    has_prev = jnp.where((b == 0) & (lay == 0), 0.0, 1.0).astype(jnp.float32)
    has_next = jnp.where((b == blocks - 1) & (lay == layers - 1), 0.0, 1.0).astype(jnp.float32)
    q3 = qphys[...].reshape(n, 8, q.shape[1])
    t3 = tphys[...].reshape(n, 8, q.shape[1])
    lower = (0.5 * q3 + conduction * t3)[:, :7]
    upper = (conduction * t3 - 0.5 * q3)[:, 1:]
    low_edge = has_prev * (0.5 * edge_r[1, 1] + conduction * edge_r[0, 1])
    high_edge = has_next * (conduction * edge_r[0, 0] - 0.5 * edge_r[1, 0])
    total = jnp.concatenate([low_edge[:, None], lower], axis=1) - 2.0 * conduction * t3
    vert[...] = total + jnp.concatenate([upper, high_edge[:, None]], axis=1)
    gathered(2)
    flux = filtered(lines(2)) * tphys[...]
    across = gradient(grad[...] - flux)
    obuf[...] = across.reshape(obuf.shape) + vert[...]

    def send_back(i, carry):
        p = lax.rem(me + i, n)
        pltpu.make_async_remote_copy(
            src_ref=obuf.at[p], dst_ref=out_ref.at[me],
            send_sem=osend_sem.at[0], recv_sem=orecv_sem.at[0],
            device_id=(p, lay), device_id_type=MESH,
        ).start()
        return carry

    lax.fori_loop(1, n, send_back, 0)
    pltpu.make_async_copy(obuf.at[me], out_ref.at[me], orecv_sem.at[0]).start()
    pltpu.make_async_copy(obuf, out_ref, orecv_sem.at[0]).wait()

    some = pl.ds(0, n - 1)
    for f in range(3):
        pltpu.make_async_copy(sbuf.at[f, some], rbuf.at[f, some], send_sem.at[f]).wait()
    pltpu.make_async_copy(obuf.at[some], out_ref.at[some], osend_sem.at[0]).wait()


def solution(mesh):
    n = mesh.shape["gx"]
    layers = mesh.shape["gz"]

    def shards(u_field, w_field, temp_field):
        ys, nx, nz = u_field.shape
        f32, mats, cut = tables(n, nx)
        f32, mats = jnp.asarray(f32), jnp.asarray(mats)
        vmem = pl.BlockSpec(memory_space=pltpu.VMEM)
        hbm = pl.BlockSpec(memory_space=pltpu.HBM)
        dma = pltpu.SemaphoreType.DMA
        back = pl.pallas_call(
            functools.partial(kernel, n, layers, cut),
            out_shape=jax.ShapeDtypeStruct((n, 8, nx), jnp.float32),
            in_specs=[hbm] * 5,
            out_specs=vmem,
            scratch_shapes=[
                pltpu.VMEM((3, ys, nx, nz), jnp.float32),
                pltpu.VMEM(f32.shape, jnp.float32),
                pltpu.VMEM(mats.shape, jnp.bfloat16),
                pltpu.VMEM((3, n, 8, nx), jnp.float32),
                pltpu.VMEM((3, n, 8, nx), jnp.float32),
                pltpu.VMEM((n, 8, nx), jnp.float32),
                pltpu.VMEM((8 * n, nx), jnp.float32),
                pltpu.VMEM((8 * n, nx), jnp.float32),
                pltpu.VMEM((8 * n, nx), jnp.float32),
                pltpu.VMEM((n, 8, nx), jnp.float32),
                pltpu.VMEM((2, 2, n, nx), jnp.float32),
                pltpu.VMEM((2, 2, n, nx), jnp.float32),
                dma((3,)), dma((2,)), dma((3,)), dma((3,)), dma((1,)), dma((1,)), dma((2, 2)), dma((2, 2)),
            ],
            compiler_params=pltpu.CompilerParams(
                collective_id=0, has_side_effects=True, vmem_limit_bytes=60 * 2**20
            ),
        )(u_field, w_field, temp_field, f32, mats)
        return jnp.swapaxes(back.reshape(ys, nz, nx), 1, 2)

    spec = P(None, "gx", "gz")
    return jax.shard_map(shards, mesh=mesh, in_specs=(spec, spec, spec), out_specs=spec, check_vma=False)
```

```python
import functools
import math

import jax
import jax.numpy as jnp
import ml_dtypes
import numpy as np
from jax import lax
from jax.experimental import pallas as pl
from jax.experimental.pallas import tpu as pltpu
from jax.sharding import PartitionSpec as P

MESH = pl.DeviceIdType.MESH
conduction = 0.3


def split_np(a):
    a32 = a.astype(np.float32)
    hi = a32.astype(ml_dtypes.bfloat16)
    lo = (a - hi.astype(np.float64)).astype(np.float32).astype(ml_dtypes.bfloat16)
    return hi, lo


@functools.lru_cache(maxsize=None)
def tables(n_dev, n_loc):
    total = n_dev * n_loc
    d = np.arange(n_dev)
    k = d[:, None] + n_dev * np.arange(-n_loc // 2, n_loc // 2)[None, :]
    kept = 3 * np.abs(k) <= total
    count = kept.sum(1)
    wide = count.max()
    assert set(count) == {wide, wide - 1}
    order = np.concatenate([d[count == wide], d[count < wide]])
    n_wide = int((count == wide).sum())
    low = np.argmax(kept, axis=1) - n_loc // 2
    centre = low + (count - 1) / 2.0
    turn = -2.0 * np.pi * (np.outer(order, d) % n_dev) / n_dev
    c, s = np.cos(turn), np.sin(turn)
    outer = np.zeros((n_dev, 2, 4, n_dev, 2, 4))
    for q in range(4):
        outer[:, 0, q, :, 0, q] = c
        outer[:, 0, q, :, 1, q] = -s
        outer[:, 1, q, :, 0, q] = s
        outer[:, 1, q, :, 1, q] = c
    outer = outer.reshape(8 * n_dev, 8 * n_dev)
    outer_inv = outer.T / n_dev
    j = np.arange(n_loc)
    apart = 2.0 * np.pi * (j[None, :] - j[:, None]) / n_loc
    step = 2.0 * np.pi / total

    def real_kernels(modes):
        kappa = np.arange(modes) - (modes - 1) / 2.0
        angle = apart[..., None] * kappa
        even = np.cos(angle).sum(-1) / n_loc
        odd = -(kappa * np.sin(angle)).sum(-1) / n_loc
        return even, odd * n_dev * step

    def frame(offset):
        turn = step * np.outer(order + n_dev * offset, j)
        return np.cos(turn), np.sin(turn), np.repeat((order + n_dev * offset)[:, None], n_loc, 1) * step

    def rows(a, signed):
        a = np.repeat(a[:, None, :], 8, axis=1)
        if signed:
            a[:, :4] *= -1.0
        return a.reshape(8 * n_dev, n_loc)

    fc, fs, fa = frame(centre[order])
    dc, ds, da = frame(np.full(n_dev, -0.5))
    f32 = np.stack([
        rows(fc, False), rows(fs, True), conduction * rows(fa, True),
        rows(dc, False), rows(ds, True), rows(da, True),
    ]).astype(np.float32)
    even_w, odd_w = real_kernels(wide)
    even_n, odd_n = real_kernels(wide - 1)
    _, full = real_kernels(n_loc)
    mats = []
    for m in (outer, outer_inv, even_w, conduction * odd_w, even_n, conduction * odd_n, full):
        mats += split_np(m)
    return f32, np.stack(mats), 8 * n_wide


def split(a):
    hi = a.astype(jnp.bfloat16)
    lo = (a - hi.astype(jnp.float32)).astype(jnp.bfloat16)
    return hi, lo


def dot(a, b):
    return jnp.dot(a, b, preferred_element_type=jnp.float32)


def kernel(
    n, layers, cut,
    u_hbm, w_hbm, t_hbm, f32_hbm, mats_hbm,
    out_ref,
    fields, tab, mats, sbuf, rbuf, obuf, grad, tphys, qphys, vert, edge_s, edge_r,
    load_sem, const_sem, send_sem, recv_sem, osend_sem, orecv_sem, esend_sem, erecv_sem,
):
    me = lax.axis_index("gx")
    lay = lax.axis_index("gz")
    blocks = n // 2
    b = lax.rem(me, blocks)
    base = me - b
    consts = [
        pltpu.make_async_copy(src, dst, const_sem.at[i])
        for i, (src, dst) in enumerate(((f32_hbm, tab), (mats_hbm, mats)))
    ]
    loads = [
        pltpu.make_async_copy(src, fields.at[f], load_sem.at[f])
        for f, src in enumerate((t_hbm, w_hbm, u_hbm))
    ]
    for c in loads + consts:
        c.start()
    nxt_gx = base + lax.rem(b + 1, blocks)
    nxt_gz = lax.rem(lay + jnp.where(b == blocks - 1, 1, 0), layers)
    prv_gx = base + lax.rem(b + blocks - 1, blocks)
    prv_gz = lax.rem(lay + jnp.where(b == 0, layers - 1, 0), layers)

    barrier = pltpu.get_barrier_semaphore()

    def greet(i, carry):
        pl.semaphore_signal(barrier, inc=1, device_id=(lax.rem(me + i, n), lay), device_id_type=MESH)
        return carry

    lax.fori_loop(1, n, greet, 0)
    pl.semaphore_signal(barrier, inc=1, device_id=(nxt_gx, nxt_gz), device_id_type=MESH)
    pl.semaphore_signal(barrier, inc=1, device_id=(prv_gx, prv_gz), device_id_type=MESH)

    def turned(f):
        loads[f].wait()
        for y in range(2):
            sbuf[f, pl.ds(y * blocks, blocks)] = fields[f, y].T.reshape(blocks, 8, fields.shape[2])

    def scatter(f):
        def send(i, carry):
            p = lax.rem(me + i, n)
            pltpu.make_async_remote_copy(
                src_ref=sbuf.at[f, p], dst_ref=rbuf.at[f, me],
                send_sem=send_sem.at[f], recv_sem=recv_sem.at[f],
                device_id=(p, lay), device_id_type=MESH,
            ).start()
            return carry

        lax.fori_loop(1, n, send, 0)
        pltpu.make_async_copy(sbuf.at[f, me], rbuf.at[f, me], recv_sem.at[f]).start()

    def gathered(f):
        pltpu.make_async_copy(sbuf.at[f], rbuf.at[f], recv_sem.at[f]).wait()

    turned(0)
    pl.semaphore_wait(barrier, n + 1)
    scatter(0)
    turned(1)
    scatter(1)
    turned(2)
    scatter(2)
    for c in consts:
        c.wait()

    def left(i, x):
        hi, lo = split(x)
        return dot(mats[i], hi) + dot(mats[i + 1], hi) + dot(mats[i], lo)

    def right(i, hi, lo):
        return dot(hi, mats[i]) + dot(lo, mats[i]) + dot(hi, mats[i + 1])

    def swapped(x):
        x3 = x.reshape(n, 8, x.shape[1])
        return jnp.concatenate([x3[:, 4:], x3[:, :4]], axis=1).reshape(x.shape)

    def modulated(x, i):
        return x * tab[i] - swapped(x) * tab[i + 1]

    def demodulated(x, i):
        return x * tab[i] + swapped(x) * tab[i + 1]

    low_cut, high_cut = cut // 16 * 16, -(-cut // 16) * 16

    def by_class(x, i):
        hi, lo = split(x)
        first = right(i, hi[:high_cut], lo[:high_cut])
        second = right(i + 4, hi[low_cut:], lo[low_cut:])
        return jnp.concatenate([first[:cut], second[cut - low_cut:]], axis=0)

    def filtered(x):
        a = modulated(left(0, x), 0)
        return left(2, demodulated(by_class(a, 4), 0))

    def filtered_and_gradient(x):
        a = modulated(left(0, x), 0)
        kept = demodulated(by_class(a, 4), 0)
        slope = demodulated(by_class(a, 6), 0) + swapped(kept) * tab[2]
        both = left(2, jnp.concatenate([kept, slope], axis=1))
        w = both.shape[1] // 2
        return both[:, :w], both[:, w:]

    def gradient(x):
        a = left(0, x)
        hi, lo = split(modulated(a, 3))
        b = demodulated(right(12, hi, lo), 3) + swapped(a) * tab[5]
        lane = lax.broadcasted_iota(jnp.int32, (8, a.shape[1]), 1)
        sign = jnp.where(lane % 2 == 0, 1.0, -1.0).astype(jnp.float32)
        total = jnp.sum(a[:8] * sign, axis=1, keepdims=True) * (math.pi / a.shape[1])
        part = lax.broadcasted_iota(jnp.int32, (8, a.shape[1]), 0)
        total = jnp.broadcast_to(total, sign.shape)
        turned_total = jnp.concatenate([total[4:], total[:4]], axis=0)
        fix = jnp.where(part < 4, -turned_total, turned_total) * sign
        b = jnp.concatenate([b[:8] + fix, b[8:]], axis=0)
        return left(2, b)

    def lines(f):
        return rbuf[f].reshape(8 * n, rbuf.shape[3])

    def edges(i, value):
        v = value.reshape(n, 8, value.shape[1])
        edge_s[i, 0] = v[:, 0]
        edge_s[i, 1] = v[:, 7]

    def edge_copies(i):
        out = []
        for side, (gx, gz) in ((0, (prv_gx, prv_gz)), (1, (nxt_gx, nxt_gz))):
            out.append(pltpu.make_async_remote_copy(
                src_ref=edge_s.at[i, side], dst_ref=edge_r.at[i, side],
                send_sem=esend_sem.at[i, side], recv_sem=erecv_sem.at[i, side],
                device_id=(gx, gz), device_id_type=MESH,
            ))
        return out

    gathered(0)
    tp, slope = filtered_and_gradient(lines(0))
    tphys[...] = tp
    grad[...] = slope
    edges(0, tp)
    t_edges = edge_copies(0)
    for c in t_edges:
        c.start()
    gathered(1)
    q = filtered(lines(1)) * tphys[...]
    qphys[...] = q
    edges(1, q)
    q_edges = edge_copies(1)
    for c in q_edges:
        c.start()
    for c in t_edges + q_edges:
        c.wait()
    has_prev = jnp.where((b == 0) & (lay == 0), 0.0, 1.0).astype(jnp.float32)
    has_next = jnp.where((b == blocks - 1) & (lay == layers - 1), 0.0, 1.0).astype(jnp.float32)
    q3 = qphys[...].reshape(n, 8, q.shape[1])
    t3 = tphys[...].reshape(n, 8, q.shape[1])
    lower = (0.5 * q3 + conduction * t3)[:, :7]
    upper = (conduction * t3 - 0.5 * q3)[:, 1:]
    low_edge = has_prev * (0.5 * edge_r[1, 1] + conduction * edge_r[0, 1])
    high_edge = has_next * (conduction * edge_r[0, 0] - 0.5 * edge_r[1, 0])
    total = jnp.concatenate([low_edge[:, None], lower], axis=1) - 2.0 * conduction * t3
    vert[...] = total + jnp.concatenate([upper, high_edge[:, None]], axis=1)
    gathered(2)
    flux = filtered(lines(2)) * tphys[...]
    across = gradient(grad[...] - flux)
    obuf[...] = across.reshape(obuf.shape) + vert[...]

    def send_back(i, carry):
        p = lax.rem(me + i, n)
        pltpu.make_async_remote_copy(
            src_ref=obuf.at[p], dst_ref=out_ref.at[me],
            send_sem=osend_sem.at[0], recv_sem=orecv_sem.at[0],
            device_id=(p, lay), device_id_type=MESH,
        ).start()
        return carry

    lax.fori_loop(1, n, send_back, 0)
    pltpu.make_async_copy(obuf.at[me], out_ref.at[me], orecv_sem.at[0]).start()
    pltpu.make_async_copy(obuf, out_ref, orecv_sem.at[0]).wait()

    some = pl.ds(0, n - 1)
    for f in range(3):
        pltpu.make_async_copy(sbuf.at[f, some], rbuf.at[f, some], send_sem.at[f]).wait()
    pltpu.make_async_copy(obuf.at[some], out_ref.at[some], osend_sem.at[0]).wait()


def solution(mesh):
    n = mesh.shape["gx"]
    layers = mesh.shape["gz"]

    def shards(u_field, w_field, temp_field):
        ys, nx, nz = u_field.shape
        f32, mats, cut = tables(n, nx)
        f32, mats = jnp.asarray(f32), jnp.asarray(mats)
        vmem = pl.BlockSpec(memory_space=pltpu.VMEM)
        hbm = pl.BlockSpec(memory_space=pltpu.HBM)
        dma = pltpu.SemaphoreType.DMA
        back = pl.pallas_call(
            functools.partial(kernel, n, layers, cut),
            out_shape=pltpu.VMEM((n, 8, nx), jnp.float32),
            in_specs=[hbm] * 5,
            out_specs=vmem,
            scratch_shapes=[
                pltpu.VMEM((3, ys, nx, nz), jnp.float32),
                pltpu.VMEM(f32.shape, jnp.float32),
                pltpu.VMEM(mats.shape, jnp.bfloat16),
                pltpu.VMEM((3, n, 8, nx), jnp.float32),
                pltpu.VMEM((3, n, 8, nx), jnp.float32),
                pltpu.VMEM((n, 8, nx), jnp.float32),
                pltpu.VMEM((8 * n, nx), jnp.float32),
                pltpu.VMEM((8 * n, nx), jnp.float32),
                pltpu.VMEM((8 * n, nx), jnp.float32),
                pltpu.VMEM((n, 8, nx), jnp.float32),
                pltpu.VMEM((2, 2, n, nx), jnp.float32),
                pltpu.VMEM((2, 2, n, nx), jnp.float32),
                dma((3,)), dma((2,)), dma((3,)), dma((3,)), dma((1,)), dma((1,)), dma((2, 2)), dma((2, 2)),
            ],
            compiler_params=pltpu.CompilerParams(
                collective_id=0, has_side_effects=True, vmem_limit_bytes=60 * 2**20
            ),
        )(u_field, w_field, temp_field, f32, mats)
        return jnp.swapaxes(back.reshape(ys, nz, nx), 1, 2)

    spec = P(None, "gx", "gz")
    return jax.shard_map(shards, mesh=mesh, in_specs=(spec, spec, spec), out_specs=spec, check_vma=False)
```

```python
import functools
import math

import jax
import jax.numpy as jnp
import ml_dtypes
import numpy as np
from jax import lax
from jax.experimental import pallas as pl
from jax.experimental.pallas import tpu as pltpu
from jax.sharding import PartitionSpec as P

MESH = pl.DeviceIdType.MESH
conduction = 0.3


def split_np(a):
    a32 = a.astype(np.float32)
    hi = a32.astype(ml_dtypes.bfloat16)
    lo = (a - hi.astype(np.float64)).astype(np.float32).astype(ml_dtypes.bfloat16)
    return hi, lo


@functools.lru_cache(maxsize=None)
def tables(n_dev, n_loc):
    total = n_dev * n_loc
    d = np.arange(n_dev)
    k = d[:, None] + n_dev * np.arange(-n_loc // 2, n_loc // 2)[None, :]
    kept = 3 * np.abs(k) <= total
    count = kept.sum(1)
    wide = count.max()
    assert set(count) == {wide, wide - 1}
    order = np.concatenate([d[count == wide], d[count < wide]])
    n_wide = int((count == wide).sum())
    low = np.argmax(kept, axis=1) - n_loc // 2
    centre = low + (count - 1) / 2.0
    turn = -2.0 * np.pi * (np.outer(order, d) % n_dev) / n_dev
    c, s = np.cos(turn), np.sin(turn)
    outer = np.zeros((n_dev, 2, 4, n_dev, 2, 4))
    for q in range(4):
        outer[:, 0, q, :, 0, q] = c
        outer[:, 0, q, :, 1, q] = -s
        outer[:, 1, q, :, 0, q] = s
        outer[:, 1, q, :, 1, q] = c
    outer = outer.reshape(8 * n_dev, 8 * n_dev)
    outer_inv = outer.T / n_dev
    j = np.arange(n_loc)
    apart = 2.0 * np.pi * (j[None, :] - j[:, None]) / n_loc
    step = 2.0 * np.pi / total

    def real_kernels(modes):
        kappa = np.arange(modes) - (modes - 1) / 2.0
        angle = apart[..., None] * kappa
        even = np.cos(angle).sum(-1) / n_loc
        odd = -(kappa * np.sin(angle)).sum(-1) / n_loc
        return even, odd * n_dev * step

    def frame(offset):
        turn = step * np.outer(order + n_dev * offset, j)
        return np.cos(turn), np.sin(turn), np.repeat((order + n_dev * offset)[:, None], n_loc, 1) * step

    def rows(a, signed):
        a = np.repeat(a[:, None, :], 8, axis=1)
        if signed:
            a[:, :4] *= -1.0
        return a.reshape(8 * n_dev, n_loc)

    fc, fs, fa = frame(centre[order])
    dc, ds, da = frame(np.full(n_dev, -0.5))
    f32 = np.stack([
        rows(fc, False), rows(fs, True), conduction * rows(fa, True),
        rows(dc, False), rows(ds, True), rows(da, True),
    ]).astype(np.float32)
    even_w, odd_w = real_kernels(wide)
    even_n, odd_n = real_kernels(wide - 1)
    _, full = real_kernels(n_loc)
    mats = []
    for m in (outer, outer_inv, even_w, conduction * odd_w, even_n, conduction * odd_n, full):
        mats += split_np(m)
    return f32, np.stack(mats), 8 * n_wide


def split(a):
    hi = a.astype(jnp.bfloat16)
    lo = (a - hi.astype(jnp.float32)).astype(jnp.bfloat16)
    return hi, lo


def dot(a, b):
    return jnp.dot(a, b, preferred_element_type=jnp.float32)


def kernel(
    n, layers, cut,
    u_hbm, w_hbm, t_hbm, f32_hbm, mats_hbm,
    out_ref,
    fields, tab, mats, sbuf, rbuf, obuf, grad, tphys, vert, edge_s, edge_r,
    load_sem, const_sem, send_sem, recv_sem, osend_sem, orecv_sem, esend_sem, erecv_sem,
):
    me = lax.axis_index("gx")
    lay = lax.axis_index("gz")
    blocks = n // 2
    b = lax.rem(me, blocks)
    base = me - b
    consts = [
        pltpu.make_async_copy(src, dst, const_sem.at[i])
        for i, (src, dst) in enumerate(((f32_hbm, tab), (mats_hbm, mats)))
    ]
    loads = [
        pltpu.make_async_copy(src, fields.at[f], load_sem.at[f])
        for f, src in enumerate((t_hbm, w_hbm, u_hbm))
    ]
    for c in loads + consts:
        c.start()
    nxt_gx = base + lax.rem(b + 1, blocks)
    nxt_gz = lax.rem(lay + jnp.where(b == blocks - 1, 1, 0), layers)
    prv_gx = base + lax.rem(b + blocks - 1, blocks)
    prv_gz = lax.rem(lay + jnp.where(b == 0, layers - 1, 0), layers)

    barrier = pltpu.get_barrier_semaphore()

    def greet(i, carry):
        pl.semaphore_signal(barrier, inc=1, device_id=(lax.rem(me + i, n), lay), device_id_type=MESH)
        return carry

    lax.fori_loop(1, n, greet, 0)
    pl.semaphore_signal(barrier, inc=1, device_id=(nxt_gx, nxt_gz), device_id_type=MESH)
    pl.semaphore_signal(barrier, inc=1, device_id=(prv_gx, prv_gz), device_id_type=MESH)

    def turned(f):
        loads[f].wait()
        for y in range(2):
            sbuf[f, pl.ds(y * blocks, blocks)] = fields[f, y].T.reshape(blocks, 8, fields.shape[2])

    def scatter(f):
        def send(i, carry):
            p = lax.rem(me + n - i, n)
            pltpu.make_async_remote_copy(
                src_ref=sbuf.at[f, p], dst_ref=rbuf.at[f, me],
                send_sem=send_sem.at[f], recv_sem=recv_sem.at[f],
                device_id=(p, lay), device_id_type=MESH,
            ).start()
            return carry

        lax.fori_loop(1, n, send, 0)
        pltpu.make_async_copy(sbuf.at[f, me], rbuf.at[f, me], recv_sem.at[f]).start()

    def gathered(f):
        pltpu.make_async_copy(sbuf.at[f], rbuf.at[f], recv_sem.at[f]).wait()

    turned(0)
    pl.semaphore_wait(barrier, n + 1)
    scatter(0)
    turned(1)
    scatter(1)
    turned(2)
    scatter(2)
    for c in consts:
        c.wait()

    def left(i, x):
        hi, lo = split(x)
        return dot(mats[i], hi) + dot(mats[i + 1], hi) + dot(mats[i], lo)

    def right(i, hi, lo):
        return dot(hi, mats[i]) + dot(lo, mats[i]) + dot(hi, mats[i + 1])

    def swapped(x):
        x3 = x.reshape(n, 8, x.shape[1])
        return jnp.concatenate([x3[:, 4:], x3[:, :4]], axis=1).reshape(x.shape)

    def modulated(x, i):
        return x * tab[i] - swapped(x) * tab[i + 1]

    def demodulated(x, i):
        return x * tab[i] + swapped(x) * tab[i + 1]

    low_cut, high_cut = cut // 16 * 16, -(-cut // 16) * 16

    def by_class(x, i):
        hi, lo = split(x)
        first = right(i, hi[:high_cut], lo[:high_cut])
        second = right(i + 4, hi[low_cut:], lo[low_cut:])
        return jnp.concatenate([first[:cut], second[cut - low_cut:]], axis=0)

    def filtered(x):
        a = modulated(left(0, x), 0)
        return left(2, demodulated(by_class(a, 4), 0))

    def filtered_and_gradient(x):
        a = modulated(left(0, x), 0)
        kept = demodulated(by_class(a, 4), 0)
        slope = demodulated(by_class(a, 6), 0) + swapped(kept) * tab[2]
        both = left(2, jnp.concatenate([kept, slope], axis=1))
        w = both.shape[1] // 2
        return both[:, :w], both[:, w:]

    def gradient_spectrum(x):
        a = left(0, x)
        hi, lo = split(modulated(a, 3))
        b = demodulated(right(12, hi, lo), 3) + swapped(a) * tab[5]
        lane = lax.broadcasted_iota(jnp.int32, (8, a.shape[1]), 1)
        sign = jnp.where(lane % 2 == 0, 1.0, -1.0).astype(jnp.float32)
        total = jnp.sum(a[:8] * sign, axis=1, keepdims=True) * (math.pi / a.shape[1])
        part = lax.broadcasted_iota(jnp.int32, (8, a.shape[1]), 0)
        total = jnp.broadcast_to(total, sign.shape)
        turned_total = jnp.concatenate([total[4:], total[:4]], axis=0)
        fix = jnp.where(part < 4, -turned_total, turned_total) * sign
        return jnp.concatenate([b[:8] + fix, b[8:]], axis=0)

    def lines(f):
        return rbuf[f].reshape(8 * n, rbuf.shape[3])

    def edges(i, value):
        v = value.reshape(n, 8, value.shape[1])
        edge_s[i, 0] = v[:, 0]
        edge_s[i, 1] = v[:, 7]

    def edge_copies(i):
        out = []
        for side, (gx, gz) in ((0, (prv_gx, prv_gz)), (1, (nxt_gx, nxt_gz))):
            out.append(pltpu.make_async_remote_copy(
                src_ref=edge_s.at[i, side], dst_ref=edge_r.at[i, side],
                send_sem=esend_sem.at[i, side], recv_sem=erecv_sem.at[i, side],
                device_id=(gx, gz), device_id_type=MESH,
            ))
        return out

    gathered(0)
    tp, slope = filtered_and_gradient(lines(0))
    tphys[...] = tp
    grad[...] = slope
    edges(0, tp)
    t_edges = edge_copies(0)
    for c in t_edges:
        c.start()
    gathered(1)
    q = filtered(lines(1)) * tphys[...]
    edges(1, q)
    q_edges = edge_copies(1)
    for c in q_edges:
        c.start()
    q3 = q.reshape(n, 8, q.shape[1])
    t3 = tphys[...].reshape(n, 8, q.shape[1])
    none = jnp.zeros((n, 1, q.shape[1]), jnp.float32)
    lower = jnp.concatenate([none, (0.5 * q3 + conduction * t3)[:, :7]], axis=1)
    higher = jnp.concatenate([(conduction * t3 - 0.5 * q3)[:, 1:], none], axis=1)
    vert[...] = lower - 2.0 * conduction * t3 + higher
    gathered(2)
    flux = filtered(lines(2)) * tphys[...]
    spec_hi, spec_lo = split(gradient_spectrum(grad[...] - flux))
    for c in t_edges + q_edges:
        c.wait()
    has_prev = jnp.where((b == 0) & (lay == 0), 0.0, 1.0).astype(jnp.float32)
    has_next = jnp.where((b == blocks - 1) & (lay == layers - 1), 0.0, 1.0).astype(jnp.float32)
    vert[:, 0] += has_prev * (0.5 * edge_r[1, 1] + conduction * edge_r[0, 1])
    vert[:, 7] += has_next * (conduction * edge_r[0, 0] - 0.5 * edge_r[1, 0])
    across = dot(mats[2], spec_hi) + dot(mats[3], spec_hi) + dot(mats[2], spec_lo)
    obuf[...] = across.reshape(obuf.shape) + vert[...]

    def send_back(i, carry):
        p = lax.rem(me + i, n)
        pltpu.make_async_remote_copy(
            src_ref=obuf.at[p], dst_ref=out_ref.at[me],
            send_sem=osend_sem.at[0], recv_sem=orecv_sem.at[0],
            device_id=(p, lay), device_id_type=MESH,
        ).start()
        return carry

    lax.fori_loop(1, n, send_back, 0)
    pltpu.make_async_copy(obuf.at[me], out_ref.at[me], orecv_sem.at[0]).start()
    pltpu.make_async_copy(obuf, out_ref, orecv_sem.at[0]).wait()

    some = pl.ds(0, n - 1)
    for f in range(3):
        pltpu.make_async_copy(sbuf.at[f, some], rbuf.at[f, some], send_sem.at[f]).wait()
    pltpu.make_async_copy(obuf.at[some], out_ref.at[some], osend_sem.at[0]).wait()


def solution(mesh):
    n = mesh.shape["gx"]
    layers = mesh.shape["gz"]

    def shards(u_field, w_field, temp_field):
        ys, nx, nz = u_field.shape
        f32, mats, cut = tables(n, nx)
        f32, mats = jnp.asarray(f32), jnp.asarray(mats)
        vmem = pl.BlockSpec(memory_space=pltpu.VMEM)
        hbm = pl.BlockSpec(memory_space=pltpu.HBM)
        dma = pltpu.SemaphoreType.DMA
        back = pl.pallas_call(
            functools.partial(kernel, n, layers, cut),
            out_shape=pltpu.VMEM((n, 8, nx), jnp.float32),
            in_specs=[hbm] * 5,
            out_specs=vmem,
            scratch_shapes=[
                pltpu.VMEM((3, ys, nx, nz), jnp.float32),
                pltpu.VMEM(f32.shape, jnp.float32),
                pltpu.VMEM(mats.shape, jnp.bfloat16),
                pltpu.VMEM((3, n, 8, nx), jnp.float32),
                pltpu.VMEM((3, n, 8, nx), jnp.float32),
                pltpu.VMEM((n, 8, nx), jnp.float32),
                pltpu.VMEM((8 * n, nx), jnp.float32),
                pltpu.VMEM((8 * n, nx), jnp.float32),
                pltpu.VMEM((n, 8, nx), jnp.float32),
                pltpu.VMEM((2, 2, n, nx), jnp.float32),
                pltpu.VMEM((2, 2, n, nx), jnp.float32),
                dma((3,)), dma((2,)), dma((3,)), dma((3,)), dma((1,)), dma((1,)), dma((2, 2)), dma((2, 2)),
            ],
            compiler_params=pltpu.CompilerParams(
                collective_id=0, has_side_effects=True, vmem_limit_bytes=60 * 2**20
            ),
        )(u_field, w_field, temp_field, f32, mats)
        return jnp.swapaxes(back.reshape(ys, nz, nx), 1, 2)

    spec = P(None, "gx", "gz")
    return jax.shard_map(shards, mesh=mesh, in_specs=(spec, spec, spec), out_specs=spec, check_vma=False)
```

```python
import functools
import math

import jax
import jax.numpy as jnp
import ml_dtypes
import numpy as np
from jax import lax
from jax.experimental import pallas as pl
from jax.experimental.pallas import tpu as pltpu
from jax.sharding import PartitionSpec as P

MESH = pl.DeviceIdType.MESH
conduction = 0.3


def split_np(a):
    a32 = a.astype(np.float32)
    hi = a32.astype(ml_dtypes.bfloat16)
    lo = (a - hi.astype(np.float64)).astype(np.float32).astype(ml_dtypes.bfloat16)
    return hi, lo


@functools.lru_cache(maxsize=None)
def tables(n_dev, n_loc):
    total = n_dev * n_loc
    d = np.arange(n_dev)
    k = d[:, None] + n_dev * np.arange(-n_loc // 2, n_loc // 2)[None, :]
    kept = 3 * np.abs(k) <= total
    count = kept.sum(1)
    wide = count.max()
    assert set(count) == {wide, wide - 1}
    order = np.concatenate([d[count == wide], d[count < wide]])
    n_wide = int((count == wide).sum())
    low = np.argmax(kept, axis=1) - n_loc // 2
    centre = low + (count - 1) / 2.0
    turn = -2.0 * np.pi * (np.outer(order, d) % n_dev) / n_dev
    c, s = np.cos(turn), np.sin(turn)
    outer = np.zeros((n_dev, 2, 4, n_dev, 2, 4))
    for q in range(4):
        outer[:, 0, q, :, 0, q] = c
        outer[:, 0, q, :, 1, q] = -s
        outer[:, 1, q, :, 0, q] = s
        outer[:, 1, q, :, 1, q] = c
    outer = outer.reshape(8 * n_dev, 8 * n_dev)
    outer_inv = outer.T / n_dev
    j = np.arange(n_loc)
    apart = 2.0 * np.pi * (j[None, :] - j[:, None]) / n_loc
    step = 2.0 * np.pi / total

    def real_kernels(modes):
        kappa = np.arange(modes) - (modes - 1) / 2.0
        angle = apart[..., None] * kappa
        even = np.cos(angle).sum(-1) / n_loc
        odd = -(kappa * np.sin(angle)).sum(-1) / n_loc
        return even, odd * n_dev * step

    def frame(offset):
        turn = step * np.outer(order + n_dev * offset, j)
        return np.cos(turn), np.sin(turn), np.repeat((order + n_dev * offset)[:, None], n_loc, 1) * step

    def rows(a, signed):
        a = np.repeat(a[:, None, :], 8, axis=1)
        if signed:
            a[:, :4] *= -1.0
        return a.reshape(8 * n_dev, n_loc)

    fc, fs, fa = frame(centre[order])
    dc, ds, da = frame(np.full(n_dev, -0.5))
    f32 = np.stack([
        rows(fc, False), rows(fs, True), conduction * rows(fa, True),
        rows(dc, False), rows(ds, True), rows(da, True),
    ]).astype(np.float32)
    even_w, odd_w = real_kernels(wide)
    even_n, odd_n = real_kernels(wide - 1)
    _, full = real_kernels(n_loc)
    mats = []
    for m in (outer, outer_inv, even_w, conduction * odd_w, even_n, conduction * odd_n, full):
        mats += split_np(m)
    return f32, np.stack(mats), 8 * n_wide


def split(a):
    hi = a.astype(jnp.bfloat16)
    lo = (a - hi.astype(jnp.float32)).astype(jnp.bfloat16)
    return hi, lo


def dot(a, b):
    return jnp.dot(a, b, preferred_element_type=jnp.float32)


def kernel(
    n, layers, cut,
    u_hbm, w_hbm, t_hbm, f32_hbm, mats_hbm,
    out_ref,
    fields, tab, mats, sbuf, rbuf, obuf, back, grad, tphys, vert, edge_s, edge_r,
    load_sem, const_sem, send_sem, recv_sem, osend_sem, orecv_sem, esend_sem, erecv_sem,
):
    me = lax.axis_index("gx")
    lay = lax.axis_index("gz")
    blocks = n // 2
    b = lax.rem(me, blocks)
    base = me - b
    consts = [
        pltpu.make_async_copy(src, dst, const_sem.at[i])
        for i, (src, dst) in enumerate(((f32_hbm, tab), (mats_hbm, mats)))
    ]
    loads = [
        pltpu.make_async_copy(src, fields.at[f], load_sem.at[f])
        for f, src in enumerate((t_hbm, w_hbm, u_hbm))
    ]
    for c in loads + consts:
        c.start()
    nxt_gx = base + lax.rem(b + 1, blocks)
    nxt_gz = lax.rem(lay + jnp.where(b == blocks - 1, 1, 0), layers)
    prv_gx = base + lax.rem(b + blocks - 1, blocks)
    prv_gz = lax.rem(lay + jnp.where(b == 0, layers - 1, 0), layers)

    barrier = pltpu.get_barrier_semaphore()

    def greet(i, carry):
        pl.semaphore_signal(barrier, inc=1, device_id=(lax.rem(me + i, n), lay), device_id_type=MESH)
        return carry

    lax.fori_loop(1, n, greet, 0)
    pl.semaphore_signal(barrier, inc=1, device_id=(nxt_gx, nxt_gz), device_id_type=MESH)
    pl.semaphore_signal(barrier, inc=1, device_id=(prv_gx, prv_gz), device_id_type=MESH)

    def turned(f):
        loads[f].wait()
        for y in range(2):
            sbuf[f, pl.ds(y * blocks, blocks)] = fields[f, y].T.reshape(blocks, 8, fields.shape[2])

    half = 4

    def to_peers(src, dst, send_s, recv_s, sign):
        def step(i, carry):
            p = lax.rem(me + n + sign * i, n)
            pltpu.make_async_remote_copy(
                src_ref=src(p), dst_ref=dst(me), send_sem=send_s, recv_sem=recv_s,
                device_id=(p, lay), device_id_type=MESH,
            ).start()
            return carry

        lax.fori_loop(1, n, step, 0)
        pltpu.make_async_copy(src(me), dst(me), recv_s).start()

    def scatter(f):
        to_peers(lambda p: sbuf.at[f, p], lambda p: rbuf.at[f, p], send_sem.at[f], recv_sem.at[f], -1)

    def scatter_half(f, c):
        part = pl.ds(half * c, half)
        to_peers(lambda p: sbuf.at[f, p, part], lambda p: rbuf.at[f, p, part], send_sem.at[f + c], recv_sem.at[f + c], -1)

    def gathered_half(f, c):
        part = pl.ds(half * c, half)
        pltpu.make_async_copy(sbuf.at[f, :, part], rbuf.at[f, :, part], recv_sem.at[f + c]).wait()

    def gathered(f):
        pltpu.make_async_copy(sbuf.at[f], rbuf.at[f], recv_sem.at[f]).wait()

    turned(0)
    pl.semaphore_wait(barrier, n + 1)
    scatter(0)
    turned(1)
    scatter(1)
    turned(2)
    scatter_half(2, 0)
    scatter_half(2, 1)
    for c in consts:
        c.wait()

    def left(i, x):
        hi, lo = split(x)
        return dot(mats[i], hi) + dot(mats[i + 1], hi) + dot(mats[i], lo)

    def right(i, hi, lo):
        return dot(hi, mats[i]) + dot(lo, mats[i]) + dot(hi, mats[i + 1])

    def swapped(x):
        x3 = x.reshape(n, 8, x.shape[1])
        return jnp.concatenate([x3[:, 4:], x3[:, :4]], axis=1).reshape(x.shape)

    def modulated(x, i):
        return x * tab[i] - swapped(x) * tab[i + 1]

    def demodulated(x, i):
        return x * tab[i] + swapped(x) * tab[i + 1]

    low_cut, high_cut = cut // 16 * 16, -(-cut // 16) * 16

    def by_class(x, i):
        hi, lo = split(x)
        first = right(i, hi[:high_cut], lo[:high_cut])
        second = right(i + 4, hi[low_cut:], lo[low_cut:])
        return jnp.concatenate([first[:cut], second[cut - low_cut:]], axis=0)

    def filtered(x):
        a = modulated(left(0, x), 0)
        return left(2, demodulated(by_class(a, 4), 0))

    def filtered_and_gradient(x):
        a = modulated(left(0, x), 0)
        kept = demodulated(by_class(a, 4), 0)
        slope = demodulated(by_class(a, 6), 0) + swapped(kept) * tab[2]
        both = left(2, jnp.concatenate([kept, slope], axis=1))
        w = both.shape[1] // 2
        return both[:, :w], both[:, w:]

    def gradient_spectrum(x):
        a = left(0, x)
        hi, lo = split(modulated(a, 3))
        b = demodulated(right(12, hi, lo), 3) + swapped(a) * tab[5]
        lane = lax.broadcasted_iota(jnp.int32, (8, a.shape[1]), 1)
        sign = jnp.where(lane % 2 == 0, 1.0, -1.0).astype(jnp.float32)
        total = jnp.sum(a[:8] * sign, axis=1, keepdims=True) * (math.pi / a.shape[1])
        part = lax.broadcasted_iota(jnp.int32, (8, a.shape[1]), 0)
        total = jnp.broadcast_to(total, sign.shape)
        turned_total = jnp.concatenate([total[4:], total[:4]], axis=0)
        fix = jnp.where(part < 4, -turned_total, turned_total) * sign
        return jnp.concatenate([b[:8] + fix, b[8:]], axis=0)

    def lines(f):
        return rbuf[f].reshape(8 * n, rbuf.shape[3])

    def edges(i, value):
        v = value.reshape(n, 8, value.shape[1])
        edge_s[i, 0] = v[:, 0]
        edge_s[i, 1] = v[:, 7]

    def edge_copies(i):
        out = []
        for side, (gx, gz) in ((0, (prv_gx, prv_gz)), (1, (nxt_gx, nxt_gz))):
            out.append(pltpu.make_async_remote_copy(
                src_ref=edge_s.at[i, side], dst_ref=edge_r.at[i, side],
                send_sem=esend_sem.at[i, side], recv_sem=erecv_sem.at[i, side],
                device_id=(gx, gz), device_id_type=MESH,
            ))
        return out

    gathered(0)
    tp, slope = filtered_and_gradient(lines(0))
    tphys[...] = tp
    grad[...] = slope
    edges(0, tp)
    t_edges = edge_copies(0)
    for c in t_edges:
        c.start()
    gathered(1)
    q = filtered(lines(1)) * tphys[...]
    edges(1, q)
    q_edges = edge_copies(1)
    for c in q_edges:
        c.start()
    q3 = q.reshape(n, 8, q.shape[1])
    t3 = tphys[...].reshape(n, 8, q.shape[1])
    none = jnp.zeros((n, 1, q.shape[1]), jnp.float32)
    lower = jnp.concatenate([none, (0.5 * q3 + conduction * t3)[:, :7]], axis=1)
    higher = jnp.concatenate([(conduction * t3 - 0.5 * q3)[:, 1:], none], axis=1)
    vert[...] = lower - 2.0 * conduction * t3 + higher
    def alone(x, c):
        zero = jnp.zeros(x.shape, x.dtype)
        parts = [x, zero] if c == 0 else [zero, x]
        return jnp.concatenate(parts, axis=1).reshape(8 * n, x.shape[2])

    def half_of(x, c):
        return x.reshape(n, 8, x.shape[-1])[:, half * c: half * c + half]

    for part in range(2):
        rows = slice(half * part, half * part + half)
        gathered_half(2, part)
        flux = half_of(filtered(alone(rbuf[2, :, rows], part)), part) * half_of(tphys[...], part)
        hi, lo = split(gradient_spectrum(alone(half_of(grad[...], part) - flux, part)))
        across = dot(mats[2], hi) + dot(mats[3], hi) + dot(mats[2], lo)
        if part == 0:
            for c in t_edges + q_edges:
                c.wait()
            has_prev = jnp.where((b == 0) & (lay == 0), 0.0, 1.0).astype(jnp.float32)
            has_next = jnp.where((b == blocks - 1) & (lay == layers - 1), 0.0, 1.0).astype(jnp.float32)
            vert[:, 0] += has_prev * (0.5 * edge_r[1, 1] + conduction * edge_r[0, 1])
            vert[:, 7] += has_next * (conduction * edge_r[0, 0] - 0.5 * edge_r[1, 0])

        done = half_of(across, part) + vert[:, rows]
        mid = done.shape[2] // 2
        obuf[part] = jnp.concatenate([done[:, :, :mid], done[:, :, mid:]], axis=1)
        to_peers(lambda p: obuf.at[part, p], lambda p: back.at[part, p], osend_sem.at[part], orecv_sem.at[0], 1)

    pltpu.make_async_copy(obuf, back, orecv_sem.at[0]).wait()
    for y in range(2):
        peers = slice(y * blocks, (y + 1) * blocks)
        cols = [
            jnp.concatenate([back[c, peers, half * side: half * side + half] for c in range(2)], axis=1)
            for side in range(2)
        ]
        lines_z = jnp.concatenate(cols, axis=2)
        out_ref[y] = lines_z.reshape(8 * blocks, lines_z.shape[2]).T

    some = pl.ds(0, n - 1)
    for f in range(2):
        pltpu.make_async_copy(sbuf.at[f, some], rbuf.at[f, some], send_sem.at[f]).wait()
    for c in range(2):
        span = pl.ds(half * c, half)
        pltpu.make_async_copy(sbuf.at[2, some, span], rbuf.at[2, some, span], send_sem.at[2 + c]).wait()
    for c in range(2):
        pltpu.make_async_copy(obuf.at[c, some], back.at[c, some], osend_sem.at[c]).wait()


def solution(mesh):
    n = mesh.shape["gx"]
    layers = mesh.shape["gz"]

    def shards(u_field, w_field, temp_field):
        ys, nx, nz = u_field.shape
        f32, mats, cut = tables(n, nx)
        f32, mats = jnp.asarray(f32), jnp.asarray(mats)
        vmem = pl.BlockSpec(memory_space=pltpu.VMEM)
        hbm = pl.BlockSpec(memory_space=pltpu.HBM)
        dma = pltpu.SemaphoreType.DMA
        return pl.pallas_call(
            functools.partial(kernel, n, layers, cut),
            out_shape=pltpu.VMEM((ys, nx, nz), jnp.float32),
            in_specs=[hbm] * 5,
            out_specs=vmem,
            scratch_shapes=[
                pltpu.VMEM((3, ys, nx, nz), jnp.float32),
                pltpu.VMEM(f32.shape, jnp.float32),
                pltpu.VMEM(mats.shape, jnp.bfloat16),
                pltpu.VMEM((3, n, 8, nx), jnp.float32),
                pltpu.VMEM((3, n, 8, nx), jnp.float32),
                pltpu.VMEM((2, n, 8, nx // 2), jnp.float32),
                pltpu.VMEM((2, n, 8, nx // 2), jnp.float32),
                pltpu.VMEM((8 * n, nx), jnp.float32),
                pltpu.VMEM((8 * n, nx), jnp.float32),
                pltpu.VMEM((n, 8, nx), jnp.float32),
                pltpu.VMEM((2, 2, n, nx), jnp.float32),
                pltpu.VMEM((2, 2, n, nx), jnp.float32),
                dma((3,)), dma((2,)), dma((4,)), dma((4,)), dma((2,)), dma((1,)), dma((2, 2)), dma((2, 2)),
            ],
            compiler_params=pltpu.CompilerParams(
                collective_id=0, has_side_effects=True, vmem_limit_bytes=60 * 2**20
            ),
        )(u_field, w_field, temp_field, f32, mats)

    spec = P(None, "gx", "gz")
    return jax.shard_map(shards, mesh=mesh, in_specs=(spec, spec, spec), out_specs=spec, check_vma=False)
```

```python
import functools
import math

import jax
import jax.numpy as jnp
import ml_dtypes
import numpy as np
from jax import lax
from jax.experimental import pallas as pl
from jax.experimental.pallas import tpu as pltpu
from jax.sharding import PartitionSpec as P

MESH = pl.DeviceIdType.MESH
conduction = 0.3


def split_np(a):
    a32 = a.astype(np.float32)
    hi = a32.astype(ml_dtypes.bfloat16)
    lo = (a - hi.astype(np.float64)).astype(np.float32).astype(ml_dtypes.bfloat16)
    return hi, lo


@functools.lru_cache(maxsize=None)
def tables(n_dev, n_loc):
    total = n_dev * n_loc
    d = np.arange(n_dev)
    k = d[:, None] + n_dev * np.arange(-n_loc // 2, n_loc // 2)[None, :]
    kept = 3 * np.abs(k) <= total
    count = kept.sum(1)
    wide = count.max()
    assert set(count) == {wide, wide - 1}
    order = np.concatenate([d[count == wide], d[count < wide]])
    n_wide = int((count == wide).sum())
    low = np.argmax(kept, axis=1) - n_loc // 2
    centre = low + (count - 1) / 2.0
    turn = -2.0 * np.pi * (np.outer(order, d) % n_dev) / n_dev
    c, s = np.cos(turn), np.sin(turn)
    outer = np.zeros((n_dev, 2, 4, n_dev, 2, 4))
    for q in range(4):
        outer[:, 0, q, :, 0, q] = c
        outer[:, 0, q, :, 1, q] = -s
        outer[:, 1, q, :, 0, q] = s
        outer[:, 1, q, :, 1, q] = c
    outer = outer.reshape(8 * n_dev, 8 * n_dev)
    outer_inv = outer.T / n_dev
    j = np.arange(n_loc)
    apart = 2.0 * np.pi * (j[None, :] - j[:, None]) / n_loc
    step = 2.0 * np.pi / total

    def real_kernels(modes):
        kappa = np.arange(modes) - (modes - 1) / 2.0
        angle = apart[..., None] * kappa
        even = np.cos(angle).sum(-1) / n_loc
        odd = -(kappa * np.sin(angle)).sum(-1) / n_loc
        return even, odd * n_dev * step

    def frame(offset):
        turn = step * np.outer(order + n_dev * offset, j)
        return np.cos(turn), np.sin(turn), np.repeat((order + n_dev * offset)[:, None], n_loc, 1) * step

    def rows(a, signed):
        a = np.repeat(a[:, None, :], 8, axis=1)
        if signed:
            a[:, :4] *= -1.0
        return a.reshape(8 * n_dev, n_loc)

    fc, fs, fa = frame(centre[order])
    dc, ds, da = frame(np.full(n_dev, -0.5))
    f32 = np.stack([
        rows(fc, False), rows(fs, True), conduction * rows(fa, True),
        rows(dc, False), rows(ds, True), rows(da, True),
    ]).astype(np.float32)
    even_w, odd_w = real_kernels(wide)
    even_n, odd_n = real_kernels(wide - 1)
    _, full = real_kernels(n_loc)
    mats = []
    for m in (outer, outer_inv, even_w, conduction * odd_w, even_n, conduction * odd_n, full):
        mats += split_np(m)
    return f32, np.stack(mats), 8 * n_wide


def split(a):
    hi = a.astype(jnp.bfloat16)
    lo = (a - hi.astype(jnp.float32)).astype(jnp.bfloat16)
    return hi, lo


def dot(a, b):
    return jnp.dot(a, b, preferred_element_type=jnp.float32)


def kernel(
    n, layers, cut,
    u_hbm, w_hbm, t_hbm, f32_hbm, mats_hbm,
    out_ref,
    fields, tab, mats, sbuf, rbuf, obuf, back, grad, tphys, vert, edge_s, edge_r,
    load_sem, const_sem, send_sem, recv_sem, osend_sem, orecv_sem, esend_sem, erecv_sem,
):
    me = lax.axis_index("gx")
    lay = lax.axis_index("gz")
    blocks = n // 2
    b = lax.rem(me, blocks)
    base = me - b
    consts = [
        pltpu.make_async_copy(src, dst, const_sem.at[i])
        for i, (src, dst) in enumerate(((f32_hbm, tab), (mats_hbm, mats)))
    ]
    loads = [
        pltpu.make_async_copy(src, fields.at[f], load_sem.at[f])
        for f, src in enumerate((t_hbm, w_hbm, u_hbm))
    ]
    for c in loads + consts:
        c.start()
    nxt_gx = base + lax.rem(b + 1, blocks)
    nxt_gz = lax.rem(lay + jnp.where(b == blocks - 1, 1, 0), layers)
    prv_gx = base + lax.rem(b + blocks - 1, blocks)
    prv_gz = lax.rem(lay + jnp.where(b == 0, layers - 1, 0), layers)

    barrier = pltpu.get_barrier_semaphore()

    def greet(i, carry):
        pl.semaphore_signal(barrier, inc=1, device_id=(lax.rem(me + i, n), lay), device_id_type=MESH)
        return carry

    lax.fori_loop(1, n, greet, 0)
    pl.semaphore_signal(barrier, inc=1, device_id=(nxt_gx, nxt_gz), device_id_type=MESH)
    pl.semaphore_signal(barrier, inc=1, device_id=(prv_gx, prv_gz), device_id_type=MESH)

    def turned(f):
        loads[f].wait()
        for y in range(2):
            sbuf[f, pl.ds(y * blocks, blocks)] = fields[f, y].T.reshape(blocks, 8, fields.shape[2])

    half = 4

    def to_peers(src, dst, send_s, recv_s, sign):
        def step(i, carry):
            p = lax.rem(me + n + (i if sign > 0 else jnp.where(i % 2 == 1, (i + 1) // 2, -(i // 2))), n)
            pltpu.make_async_remote_copy(
                src_ref=src(p), dst_ref=dst(me), send_sem=send_s, recv_sem=recv_s,
                device_id=(p, lay), device_id_type=MESH,
            ).start()
            return carry

        lax.fori_loop(1, n, step, 0)
        pltpu.make_async_copy(src(me), dst(me), recv_s).start()

    def scatter(f):
        to_peers(lambda p: sbuf.at[f, p], lambda p: rbuf.at[f, p], send_sem.at[f], recv_sem.at[f], -1)

    def scatter_half(f, c):
        part = pl.ds(half * c, half)
        to_peers(lambda p: sbuf.at[f, p, part], lambda p: rbuf.at[f, p, part], send_sem.at[f + c], recv_sem.at[f + c], -1)

    def gathered_half(f, c):
        part = pl.ds(half * c, half)
        pltpu.make_async_copy(sbuf.at[f, :, part], rbuf.at[f, :, part], recv_sem.at[f + c]).wait()

    def gathered(f):
        pltpu.make_async_copy(sbuf.at[f], rbuf.at[f], recv_sem.at[f]).wait()

    turned(0)
    pl.semaphore_wait(barrier, n + 1)
    scatter(0)
    turned(1)
    scatter(1)
    turned(2)
    scatter_half(2, 0)
    scatter_half(2, 1)
    for c in consts:
        c.wait()

    def left(i, x):
        hi, lo = split(x)
        return dot(mats[i], hi) + dot(mats[i + 1], hi) + dot(mats[i], lo)

    def right(i, hi, lo):
        return dot(hi, mats[i]) + dot(lo, mats[i]) + dot(hi, mats[i + 1])

    def swapped(x):
        x3 = x.reshape(n, 8, x.shape[1])
        return jnp.concatenate([x3[:, 4:], x3[:, :4]], axis=1).reshape(x.shape)

    def modulated(x, i):
        return x * tab[i] - swapped(x) * tab[i + 1]

    def demodulated(x, i):
        return x * tab[i] + swapped(x) * tab[i + 1]

    low_cut, high_cut = cut // 16 * 16, -(-cut // 16) * 16

    def by_class(x, i):
        hi, lo = split(x)
        first = right(i, hi[:high_cut], lo[:high_cut])
        second = right(i + 4, hi[low_cut:], lo[low_cut:])
        return jnp.concatenate([first[:cut], second[cut - low_cut:]], axis=0)

    def filtered(x):
        a = modulated(left(0, x), 0)
        return left(2, demodulated(by_class(a, 4), 0))

    def filtered_and_gradient(x):
        a = modulated(left(0, x), 0)
        kept = demodulated(by_class(a, 4), 0)
        slope = demodulated(by_class(a, 6), 0) + swapped(kept) * tab[2]
        both = left(2, jnp.concatenate([kept, slope], axis=1))
        w = both.shape[1] // 2
        return both[:, :w], both[:, w:]

    def gradient_spectrum(x):
        a = left(0, x)
        hi, lo = split(modulated(a, 3))
        b = demodulated(right(12, hi, lo), 3) + swapped(a) * tab[5]
        lane = lax.broadcasted_iota(jnp.int32, (8, a.shape[1]), 1)
        sign = jnp.where(lane % 2 == 0, 1.0, -1.0).astype(jnp.float32)
        total = jnp.sum(a[:8] * sign, axis=1, keepdims=True) * (math.pi / a.shape[1])
        part = lax.broadcasted_iota(jnp.int32, (8, a.shape[1]), 0)
        total = jnp.broadcast_to(total, sign.shape)
        turned_total = jnp.concatenate([total[4:], total[:4]], axis=0)
        fix = jnp.where(part < 4, -turned_total, turned_total) * sign
        return jnp.concatenate([b[:8] + fix, b[8:]], axis=0)

    def lines(f):
        return rbuf[f].reshape(8 * n, rbuf.shape[3])

    def edges(i, value):
        v = value.reshape(n, 8, value.shape[1])
        edge_s[i, 0] = v[:, 0]
        edge_s[i, 1] = v[:, 7]

    def edge_copies(i):
        out = []
        for side, (gx, gz) in ((0, (prv_gx, prv_gz)), (1, (nxt_gx, nxt_gz))):
            out.append(pltpu.make_async_remote_copy(
                src_ref=edge_s.at[i, side], dst_ref=edge_r.at[i, side],
                send_sem=esend_sem.at[i, side], recv_sem=erecv_sem.at[i, side],
                device_id=(gx, gz), device_id_type=MESH,
            ))
        return out

    gathered(0)
    tp, slope = filtered_and_gradient(lines(0))
    tphys[...] = tp
    grad[...] = slope
    edges(0, tp)
    t_edges = edge_copies(0)
    for c in t_edges:
        c.start()
    gathered(1)
    q = filtered(lines(1)) * tphys[...]
    edges(1, q)
    q_edges = edge_copies(1)
    for c in q_edges:
        c.start()
    q3 = q.reshape(n, 8, q.shape[1])
    t3 = tphys[...].reshape(n, 8, q.shape[1])
    none = jnp.zeros((n, 1, q.shape[1]), jnp.float32)
    lower = jnp.concatenate([none, (0.5 * q3 + conduction * t3)[:, :7]], axis=1)
    higher = jnp.concatenate([(conduction * t3 - 0.5 * q3)[:, 1:], none], axis=1)
    vert[...] = lower - 2.0 * conduction * t3 + higher
    def alone(x, c):
        zero = jnp.zeros(x.shape, x.dtype)
        parts = [x, zero] if c == 0 else [zero, x]
        return jnp.concatenate(parts, axis=1).reshape(8 * n, x.shape[2])

    def half_of(x, c):
        return x.reshape(n, 8, x.shape[-1])[:, half * c: half * c + half]

    for part in range(2):
        rows = slice(half * part, half * part + half)
        gathered_half(2, part)
        flux = half_of(filtered(alone(rbuf[2, :, rows], part)), part) * half_of(tphys[...], part)
        hi, lo = split(gradient_spectrum(alone(half_of(grad[...], part) - flux, part)))
        across = dot(mats[2], hi) + dot(mats[3], hi) + dot(mats[2], lo)
        if part == 0:
            for c in t_edges + q_edges:
                c.wait()
            has_prev = jnp.where((b == 0) & (lay == 0), 0.0, 1.0).astype(jnp.float32)
            has_next = jnp.where((b == blocks - 1) & (lay == layers - 1), 0.0, 1.0).astype(jnp.float32)
            vert[:, 0] += has_prev * (0.5 * edge_r[1, 1] + conduction * edge_r[0, 1])
            vert[:, 7] += has_next * (conduction * edge_r[0, 0] - 0.5 * edge_r[1, 0])

        done = half_of(across, part) + vert[:, rows]
        mid = done.shape[2] // 2
        obuf[part] = jnp.concatenate([done[:, :, :mid], done[:, :, mid:]], axis=1)
        to_peers(lambda p: obuf.at[part, p], lambda p: back.at[part, p], osend_sem.at[part], orecv_sem.at[0], 1)

    pltpu.make_async_copy(obuf, back, orecv_sem.at[0]).wait()
    for y in range(2):
        peers = slice(y * blocks, (y + 1) * blocks)
        cols = [
            jnp.concatenate([back[c, peers, half * side: half * side + half] for c in range(2)], axis=1)
            for side in range(2)
        ]
        lines_z = jnp.concatenate(cols, axis=2)
        out_ref[y] = lines_z.reshape(8 * blocks, lines_z.shape[2]).T

    some = pl.ds(0, n - 1)
    for f in range(2):
        pltpu.make_async_copy(sbuf.at[f, some], rbuf.at[f, some], send_sem.at[f]).wait()
    for c in range(2):
        span = pl.ds(half * c, half)
        pltpu.make_async_copy(sbuf.at[2, some, span], rbuf.at[2, some, span], send_sem.at[2 + c]).wait()
    for c in range(2):
        pltpu.make_async_copy(obuf.at[c, some], back.at[c, some], osend_sem.at[c]).wait()


def solution(mesh):
    n = mesh.shape["gx"]
    layers = mesh.shape["gz"]

    def shards(u_field, w_field, temp_field):
        ys, nx, nz = u_field.shape
        f32, mats, cut = tables(n, nx)
        f32, mats = jnp.asarray(f32), jnp.asarray(mats)
        vmem = pl.BlockSpec(memory_space=pltpu.VMEM)
        hbm = pl.BlockSpec(memory_space=pltpu.HBM)
        dma = pltpu.SemaphoreType.DMA
        return pl.pallas_call(
            functools.partial(kernel, n, layers, cut),
            out_shape=pltpu.VMEM((ys, nx, nz), jnp.float32),
            in_specs=[hbm] * 5,
            out_specs=vmem,
            scratch_shapes=[
                pltpu.VMEM((3, ys, nx, nz), jnp.float32),
                pltpu.VMEM(f32.shape, jnp.float32),
                pltpu.VMEM(mats.shape, jnp.bfloat16),
                pltpu.VMEM((3, n, 8, nx), jnp.float32),
                pltpu.VMEM((3, n, 8, nx), jnp.float32),
                pltpu.VMEM((2, n, 8, nx // 2), jnp.float32),
                pltpu.VMEM((2, n, 8, nx // 2), jnp.float32),
                pltpu.VMEM((8 * n, nx), jnp.float32),
                pltpu.VMEM((8 * n, nx), jnp.float32),
                pltpu.VMEM((n, 8, nx), jnp.float32),
                pltpu.VMEM((2, 2, n, nx), jnp.float32),
                pltpu.VMEM((2, 2, n, nx), jnp.float32),
                dma((3,)), dma((2,)), dma((4,)), dma((4,)), dma((2,)), dma((1,)), dma((2, 2)), dma((2, 2)),
            ],
            compiler_params=pltpu.CompilerParams(
                collective_id=0, has_side_effects=True, vmem_limit_bytes=60 * 2**20
            ),
        )(u_field, w_field, temp_field, f32, mats)

    spec = P(None, "gx", "gz")
    return jax.shard_map(shards, mesh=mesh, in_specs=(spec, spec, spec), out_specs=spec, check_vma=False)
```

```python
import functools
import math

import jax
import jax.numpy as jnp
import ml_dtypes
import numpy as np
from jax import lax
from jax.experimental import pallas as pl
from jax.experimental.pallas import tpu as pltpu
from jax.sharding import PartitionSpec as P

MESH = pl.DeviceIdType.MESH
conduction = 0.3


def split_np(a):
    a32 = a.astype(np.float32)
    hi = a32.astype(ml_dtypes.bfloat16)
    lo = (a - hi.astype(np.float64)).astype(np.float32).astype(ml_dtypes.bfloat16)
    return hi, lo


@functools.lru_cache(maxsize=None)
def tables(n_dev, n_loc):
    total = n_dev * n_loc
    d = np.arange(n_dev)
    k = d[:, None] + n_dev * np.arange(-n_loc // 2, n_loc // 2)[None, :]
    kept = 3 * np.abs(k) <= total
    count = kept.sum(1)
    wide = count.max()
    assert set(count) == {wide, wide - 1}
    order = np.concatenate([d[count == wide], d[count < wide]])
    n_wide = int((count == wide).sum())
    low = np.argmax(kept, axis=1) - n_loc // 2
    centre = low + (count - 1) / 2.0
    turn = -2.0 * np.pi * (np.outer(order, d) % n_dev) / n_dev
    c, s = np.cos(turn), np.sin(turn)
    outer = np.zeros((n_dev, 2, 4, n_dev, 2, 4))
    for q in range(4):
        outer[:, 0, q, :, 0, q] = c
        outer[:, 0, q, :, 1, q] = -s
        outer[:, 1, q, :, 0, q] = s
        outer[:, 1, q, :, 1, q] = c
    outer = outer.reshape(8 * n_dev, 8 * n_dev)
    outer_inv = outer.T / n_dev
    j = np.arange(n_loc)
    apart = 2.0 * np.pi * (j[None, :] - j[:, None]) / n_loc
    step = 2.0 * np.pi / total

    def real_kernels(modes):
        kappa = np.arange(modes) - (modes - 1) / 2.0
        angle = apart[..., None] * kappa
        even = np.cos(angle).sum(-1) / n_loc
        odd = -(kappa * np.sin(angle)).sum(-1) / n_loc
        return even, odd * n_dev * step

    def frame(offset):
        turn = step * np.outer(order + n_dev * offset, j)
        return np.cos(turn), np.sin(turn), np.repeat((order + n_dev * offset)[:, None], n_loc, 1) * step

    def rows(a, signed):
        a = np.repeat(a[:, None, :], 8, axis=1)
        if signed:
            a[:, :4] *= -1.0
        return a.reshape(8 * n_dev, n_loc)

    fc, fs, fa = frame(centre[order])
    dc, ds, da = frame(np.full(n_dev, -0.5))
    f32 = np.stack([
        rows(fc, False), rows(fs, True), conduction * rows(fa, True),
        rows(dc, False), rows(ds, True), rows(da, True),
    ]).astype(np.float32)
    even_w, odd_w = real_kernels(wide)
    even_n, odd_n = real_kernels(wide - 1)
    _, full = real_kernels(n_loc)
    mats = []
    for m in (outer, outer_inv, even_w, conduction * odd_w, even_n, conduction * odd_n, full):
        mats += split_np(m)
    return f32, np.stack(mats), 8 * n_wide


def split(a):
    hi = a.astype(jnp.bfloat16)
    lo = (a - hi.astype(jnp.float32)).astype(jnp.bfloat16)
    return hi, lo


def dot(a, b):
    return jnp.dot(a, b, preferred_element_type=jnp.float32)


def kernel(
    n, layers, cut,
    u_hbm, w_hbm, t_hbm, f32_hbm, mats_hbm,
    out_ref,
    fields, tab, mats, sbuf, rbuf, obuf, back, grad, tphys, vert, edge_s, edge_r,
    load_sem, const_sem, send_sem, recv_sem, osend_sem, orecv_sem, esend_sem, erecv_sem,
):
    me = lax.axis_index("gx")
    lay = lax.axis_index("gz")
    blocks = n // 2
    b = lax.rem(me, blocks)
    base = me - b
    consts = [
        pltpu.make_async_copy(src, dst, const_sem.at[i])
        for i, (src, dst) in enumerate(((f32_hbm, tab), (mats_hbm, mats)))
    ]
    loads = [
        pltpu.make_async_copy(src, fields.at[f], load_sem.at[f])
        for f, src in enumerate((t_hbm, w_hbm, u_hbm))
    ]
    loads[0].start()
    nxt_gx = base + lax.rem(b + 1, blocks)
    nxt_gz = lax.rem(lay + jnp.where(b == blocks - 1, 1, 0), layers)
    prv_gx = base + lax.rem(b + blocks - 1, blocks)
    prv_gz = lax.rem(lay + jnp.where(b == 0, layers - 1, 0), layers)

    barrier = pltpu.get_barrier_semaphore()

    def greet(i, carry):
        pl.semaphore_signal(barrier, inc=1, device_id=(lax.rem(me + i, n), lay), device_id_type=MESH)
        return carry

    lax.fori_loop(1, n, greet, 0)
    pl.semaphore_signal(barrier, inc=1, device_id=(nxt_gx, nxt_gz), device_id_type=MESH)
    pl.semaphore_signal(barrier, inc=1, device_id=(prv_gx, prv_gz), device_id_type=MESH)

    for c in loads[1:] + consts:
        c.start()

    def turned(f):
        loads[f].wait()
        for y in range(2):
            sbuf[f, pl.ds(y * blocks, blocks)] = fields[f, y].T.reshape(blocks, 8, fields.shape[2])

    half = 4

    def to_peers(src, dst, send_s, recv_s, sign):
        def step(i, carry):
            p = lax.rem(me + n + (i if sign > 0 else jnp.where(i % 2 == 1, (i + 1) // 2, -(i // 2))), n)
            pltpu.make_async_remote_copy(
                src_ref=src(p), dst_ref=dst(me), send_sem=send_s, recv_sem=recv_s,
                device_id=(p, lay), device_id_type=MESH,
            ).start()
            return carry

        lax.fori_loop(1, n, step, 0)
        pltpu.make_async_copy(src(me), dst(me), recv_s).start()

    def scatter(f):
        to_peers(lambda p: sbuf.at[f, p], lambda p: rbuf.at[f, p], send_sem.at[f], recv_sem.at[f], -1)

    def scatter_half(f, c):
        part = pl.ds(half * c, half)
        to_peers(lambda p: sbuf.at[f, p, part], lambda p: rbuf.at[f, p, part], send_sem.at[f + c], recv_sem.at[f + c], -1)

    def gathered_half(f, c):
        part = pl.ds(half * c, half)
        pltpu.make_async_copy(sbuf.at[f, :, part], rbuf.at[f, :, part], recv_sem.at[f + c]).wait()

    def gathered(f):
        pltpu.make_async_copy(sbuf.at[f], rbuf.at[f], recv_sem.at[f]).wait()

    turned(0)
    pl.semaphore_wait(barrier, n + 1)
    scatter(0)
    turned(1)
    scatter(1)
    turned(2)
    scatter_half(2, 0)
    scatter_half(2, 1)
    for c in consts:
        c.wait()

    def left(i, x):
        hi, lo = split(x)
        return dot(mats[i], hi) + dot(mats[i + 1], hi) + dot(mats[i], lo)

    def right(i, hi, lo):
        return dot(hi, mats[i]) + dot(lo, mats[i]) + dot(hi, mats[i + 1])

    def swapped(x):
        x3 = x.reshape(n, 8, x.shape[1])
        return jnp.concatenate([x3[:, 4:], x3[:, :4]], axis=1).reshape(x.shape)

    def modulated(x, i):
        return x * tab[i] - swapped(x) * tab[i + 1]

    def demodulated(x, i):
        return x * tab[i] + swapped(x) * tab[i + 1]

    low_cut, high_cut = cut // 16 * 16, -(-cut // 16) * 16

    def by_class(x, i):
        hi, lo = split(x)
        first = right(i, hi[:high_cut], lo[:high_cut])
        second = right(i + 4, hi[low_cut:], lo[low_cut:])
        return jnp.concatenate([first[:cut], second[cut - low_cut:]], axis=0)

    def filtered(x):
        a = modulated(left(0, x), 0)
        return left(2, demodulated(by_class(a, 4), 0))

    def filtered_and_gradient(x):
        a = modulated(left(0, x), 0)
        kept = demodulated(by_class(a, 4), 0)
        slope = demodulated(by_class(a, 6), 0) + swapped(kept) * tab[2]
        both = left(2, jnp.concatenate([kept, slope], axis=1))
        w = both.shape[1] // 2
        return both[:, :w], both[:, w:]

    def gradient_spectrum(x):
        a = left(0, x)
        hi, lo = split(modulated(a, 3))
        b = demodulated(right(12, hi, lo), 3) + swapped(a) * tab[5]
        lane = lax.broadcasted_iota(jnp.int32, (8, a.shape[1]), 1)
        sign = jnp.where(lane % 2 == 0, 1.0, -1.0).astype(jnp.float32)
        total = jnp.sum(a[:8] * sign, axis=1, keepdims=True) * (math.pi / a.shape[1])
        part = lax.broadcasted_iota(jnp.int32, (8, a.shape[1]), 0)
        total = jnp.broadcast_to(total, sign.shape)
        turned_total = jnp.concatenate([total[4:], total[:4]], axis=0)
        fix = jnp.where(part < 4, -turned_total, turned_total) * sign
        return jnp.concatenate([b[:8] + fix, b[8:]], axis=0)

    def lines(f):
        return rbuf[f].reshape(8 * n, rbuf.shape[3])

    def edges(i, value):
        v = value.reshape(n, 8, value.shape[1])
        edge_s[i, 0] = v[:, 0]
        edge_s[i, 1] = v[:, 7]

    def edge_copies(i):
        out = []
        for side, (gx, gz) in ((0, (prv_gx, prv_gz)), (1, (nxt_gx, nxt_gz))):
            out.append(pltpu.make_async_remote_copy(
                src_ref=edge_s.at[i, side], dst_ref=edge_r.at[i, side],
                send_sem=esend_sem.at[i, side], recv_sem=erecv_sem.at[i, side],
                device_id=(gx, gz), device_id_type=MESH,
            ))
        return out

    gathered(0)
    tp, slope = filtered_and_gradient(lines(0))
    tphys[...] = tp
    grad[...] = slope
    edges(0, tp)
    t_edges = edge_copies(0)
    for c in t_edges:
        c.start()
    gathered(1)
    q = filtered(lines(1)) * tphys[...]
    edges(1, q)
    q_edges = edge_copies(1)
    for c in q_edges:
        c.start()
    q3 = q.reshape(n, 8, q.shape[1])
    t3 = tphys[...].reshape(n, 8, q.shape[1])
    none = jnp.zeros((n, 1, q.shape[1]), jnp.float32)
    lower = jnp.concatenate([none, (0.5 * q3 + conduction * t3)[:, :7]], axis=1)
    higher = jnp.concatenate([(conduction * t3 - 0.5 * q3)[:, 1:], none], axis=1)
    vert[...] = lower - 2.0 * conduction * t3 + higher
    def alone(x, c):
        zero = jnp.zeros(x.shape, x.dtype)
        parts = [x, zero] if c == 0 else [zero, x]
        return jnp.concatenate(parts, axis=1).reshape(8 * n, x.shape[2])

    def half_of(x, c):
        return x.reshape(n, 8, x.shape[-1])[:, half * c: half * c + half]

    for part in range(2):
        rows = slice(half * part, half * part + half)
        gathered_half(2, part)
        flux = half_of(filtered(alone(rbuf[2, :, rows], part)), part) * half_of(tphys[...], part)
        hi, lo = split(gradient_spectrum(alone(half_of(grad[...], part) - flux, part)))
        across = dot(mats[2], hi) + dot(mats[3], hi) + dot(mats[2], lo)
        if part == 0:
            for c in t_edges + q_edges:
                c.wait()
            has_prev = jnp.where((b == 0) & (lay == 0), 0.0, 1.0).astype(jnp.float32)
            has_next = jnp.where((b == blocks - 1) & (lay == layers - 1), 0.0, 1.0).astype(jnp.float32)
            vert[:, 0] += has_prev * (0.5 * edge_r[1, 1] + conduction * edge_r[0, 1])
            vert[:, 7] += has_next * (conduction * edge_r[0, 0] - 0.5 * edge_r[1, 0])

        done = half_of(across, part) + vert[:, rows]
        mid = done.shape[2] // 2
        obuf[part] = jnp.concatenate([done[:, :, :mid], done[:, :, mid:]], axis=1)
        to_peers(lambda p: obuf.at[part, p], lambda p: back.at[part, p], osend_sem.at[part], orecv_sem.at[0], 1)

    pltpu.make_async_copy(obuf, back, orecv_sem.at[0]).wait()
    for y in range(2):
        peers = slice(y * blocks, (y + 1) * blocks)
        cols = [
            jnp.concatenate([back[c, peers, half * side: half * side + half] for c in range(2)], axis=1)
            for side in range(2)
        ]
        lines_z = jnp.concatenate(cols, axis=2)
        out_ref[y] = lines_z.reshape(8 * blocks, lines_z.shape[2]).T

    some = pl.ds(0, n - 1)
    for f in range(2):
        pltpu.make_async_copy(sbuf.at[f, some], rbuf.at[f, some], send_sem.at[f]).wait()
    for c in range(2):
        span = pl.ds(half * c, half)
        pltpu.make_async_copy(sbuf.at[2, some, span], rbuf.at[2, some, span], send_sem.at[2 + c]).wait()
    for c in range(2):
        pltpu.make_async_copy(obuf.at[c, some], back.at[c, some], osend_sem.at[c]).wait()


def solution(mesh):
    n = mesh.shape["gx"]
    layers = mesh.shape["gz"]

    def shards(u_field, w_field, temp_field):
        ys, nx, nz = u_field.shape
        f32, mats, cut = tables(n, nx)
        f32, mats = jnp.asarray(f32), jnp.asarray(mats)
        vmem = pl.BlockSpec(memory_space=pltpu.VMEM)
        hbm = pl.BlockSpec(memory_space=pltpu.HBM)
        dma = pltpu.SemaphoreType.DMA
        return pl.pallas_call(
            functools.partial(kernel, n, layers, cut),
            out_shape=pltpu.VMEM((ys, nx, nz), jnp.float32),
            in_specs=[hbm] * 5,
            out_specs=vmem,
            scratch_shapes=[
                pltpu.VMEM((3, ys, nx, nz), jnp.float32),
                pltpu.VMEM(f32.shape, jnp.float32),
                pltpu.VMEM(mats.shape, jnp.bfloat16),
                pltpu.VMEM((3, n, 8, nx), jnp.float32),
                pltpu.VMEM((3, n, 8, nx), jnp.float32),
                pltpu.VMEM((2, n, 8, nx // 2), jnp.float32),
                pltpu.VMEM((2, n, 8, nx // 2), jnp.float32),
                pltpu.VMEM((8 * n, nx), jnp.float32),
                pltpu.VMEM((8 * n, nx), jnp.float32),
                pltpu.VMEM((n, 8, nx), jnp.float32),
                pltpu.VMEM((2, 2, n, nx), jnp.float32),
                pltpu.VMEM((2, 2, n, nx), jnp.float32),
                dma((3,)), dma((2,)), dma((4,)), dma((4,)), dma((2,)), dma((1,)), dma((2, 2)), dma((2, 2)),
            ],
            compiler_params=pltpu.CompilerParams(
                collective_id=0, has_side_effects=True, vmem_limit_bytes=60 * 2**20
            ),
        )(u_field, w_field, temp_field, f32, mats)

    spec = P(None, "gx", "gz")
    return jax.shard_map(shards, mesh=mesh, in_specs=(spec, spec, spec), out_specs=spec, check_vma=False)
```
